512 devices in a mesh: ctx: 64 (over x_hi, z, core), grp: 8 (over x_lo, y).
Axes of the slice: x: 4 (x_hi: 2, x_lo: 2; x = x_hi * 2 + x_lo), y: 4, z: 16, core: 2. Of those that a mesh axis runs over, the one named last changes fastest.
Arguments:
- query_states: bfloat16 [8, 8192, 2048], P('grp', 'ctx'), may hold values from -2 to 2
- key_states: bfloat16 [8, 8192, 512], P('grp', 'ctx'), may hold values from -2 to 2
- value_states: bfloat16 [8, 8192, 512], P('grp', 'ctx'), may hold values from -6 to 6
- lengths: int32 [8], P('grp'), may hold values from 2048 to 8192, as said below
- queue_keys: bfloat16 [131072, 2048], P(('ctx', 'grp')), may hold values from -0.11481983 to 0.11481983
- write_pos: int32 [8], replicated, may hold values from 0 to 131071, as said below
- teacher: float32 [8, 131072], P(None, ('ctx', 'grp')), may hold values from -12 to 12
Outputs:
- loss_value: float32 [], replicated
- embedding: float32 [8, 2048], P('grp')
- grad_query: bfloat16 [8, 8192, 2048], P('grp', 'ctx')
- grad_key: bfloat16 [8, 8192, 512], P('grp', 'ctx')
- grad_value: bfloat16 [8, 8192, 512], P('grp', 'ctx')
The draws below stay inside these ranges and needn't reach their ends.
Inputs may be any that keep to these rules, and one draw needn't show every extreme that they name: `lengths`: some document is full. `write_pos`: distinct entries.
All inputs are finite; a program needn't handle non-finite values.
Results may differ from the reference program's by a relative error of at most 0.0079.
Values may be sent and summed in bfloat16 or wider, within the bound.
A program may use at most 64 MiB of HBM per device.

```python
import math
import jax
import jax.numpy as jnp
from jax import lax

HQ = 16
HK = 4
HD = 128
SPAN = 2
SEQ_DEV = 128
E = 2048
WINDOW = 256
LEN = 8192
DOCS = 8
QUEUE = 131072
N_CTX = 64


def draw_lengths(key, part):
    key = jax.random.fold_in(key, 11)
    lead_key, pick_key = jax.random.split(key)
    drawn_lengths = jax.random.randint(lead_key, (DOCS,), LEN // 4, LEN + 1)
    chosen = jax.random.randint(pick_key, (), 0, DOCS)
    return drawn_lengths.at[chosen].set(LEN).astype(jnp.int32)


def draw_write_pos(key, part):
    key = jax.random.fold_in(key, 23)
    lead_key, pick_key = jax.random.split(key)
    shuffled = jax.random.permutation(lead_key, QUEUE - 1)[:DOCS]
    chosen = jax.random.randint(pick_key, (), 0, DOCS)
    return shuffled.at[chosen].set(QUEUE - 1).astype(jnp.int32)


def draw_queue_keys(key, part):
    key = jax.random.fold_in(key, 37)
    lead_key, scale_key = jax.random.split(key, 2)
    entries = jax.random.uniform(lead_key, (QUEUE, E), jnp.float32, -1.0, 1.0)
    row_scale = jnp.exp(jax.random.uniform(scale_key, (QUEUE, 1), jnp.float32, math.log(0.3), math.log(3.0)))
    return (entries * row_scale * (3.0 / E) ** 0.5).astype(jnp.bfloat16)


def shard_levels(stream_key, extent, cuts, low, high):
    loudness = 1.0
    for axis_at, blocks in cuts:
        draws = jax.random.uniform(jax.random.fold_in(jax.random.fold_in(stream_key, 6), axis_at), (blocks,), jnp.float32, low / len(cuts), high / len(cuts))
        loudness = loudness * jnp.repeat(jnp.exp(draws), extent[axis_at] // blocks).reshape((-1,) + (1,) * (len(extent) - 1 - axis_at))
    return loudness


def normal_values(rng, dims, scale, bound, cuts=(), kind=jnp.bfloat16):
    values = scale * jax.random.normal(rng, dims, jnp.float32)
    if cuts:
        values = values * shard_levels(rng, dims, cuts, -0.22, 0.18)
    return jnp.clip(values, -bound, bound).astype(kind)


def setup_inputs(seed: int = 0) -> dict:
    arg_keys = jax.random.split(jax.random.key(seed), 8)
    return {
        "query_states": jnp.clip(jax.random.uniform(arg_keys[0], (DOCS, LEN, HQ * HD), jnp.float32, -2.0, 2.0) * shard_levels(arg_keys[0], (DOCS, LEN, HQ * HD), ((0, 8), (1, 64)), -0.4, 0.0), -2.0, 2.0).astype(jnp.bfloat16),
        "key_states": jnp.clip(jax.random.uniform(arg_keys[1], (DOCS, LEN, HK * HD), jnp.float32, -2.0, 2.0) * shard_levels(arg_keys[1], (DOCS, LEN, HK * HD), ((0, 8), (1, 64)), -0.4, 0.0), -2.0, 2.0).astype(jnp.bfloat16),
        "value_states": normal_values(arg_keys[2], (DOCS, LEN, HK * HD), 1.0, 6.0, ((0, 8), (1, 64))),
        "lengths": draw_lengths(jax.random.fold_in(arg_keys[7], 71), 0),
        "queue_keys": draw_queue_keys(jax.random.fold_in(arg_keys[7], 71), 0),
        "write_pos": draw_write_pos(jax.random.fold_in(arg_keys[7], 71), 0),
        "teacher": normal_values(arg_keys[6], (DOCS, QUEUE), 3.0, 12.0, ((1, 512),), jnp.float32),
    }


inverse_temp = 10.0
loss_scale = 2.0 ** 24
norm_eps = 1e-06

def rounded(values):
    return lax.optimization_barrier(values.astype(jnp.bfloat16)).astype(jnp.float32)

def padded_states(states):
    padding = jnp.zeros((SPAN * SEQ_DEV, states.shape[1]), states.dtype)
    return jnp.concatenate([padding, states], 0).reshape(-1, HK, HD)

def block_state(query_doc, keys_all, values_all, block_index, length):
    row_count = SEQ_DEV
    row_start = block_index * row_count
    query_block = lax.dynamic_slice_in_dim(query_doc, row_start, row_count, 0)
    key_tile = lax.dynamic_slice_in_dim(keys_all, row_start, (SPAN + 1) * row_count, 0).astype(jnp.float32)
    value_tile = lax.dynamic_slice_in_dim(values_all, row_start, (SPAN + 1) * row_count, 0).astype(jnp.float32)
    grouped = query_block.reshape(row_count, HK, HQ // HK, HD).astype(jnp.float32)
    scores = jnp.einsum('qkgh,tkh->kgqt', grouped, key_tile) * HD ** (-0.5)
    query_pos = row_start + jnp.arange(row_count, dtype=jnp.int32)
    key_pos = row_start - SPAN * row_count + jnp.arange((SPAN + 1) * row_count, dtype=jnp.int32)
    visible = (key_pos[None, :] <= query_pos[:, None]) & (key_pos[None, :] > query_pos[:, None] - WINDOW) & (key_pos[None, :] >= 0)
    weight = jnp.where(visible, jnp.exp(scores), 0.0)
    denominator = lax.optimization_barrier(jnp.sum(weight, -1))
    output = jnp.einsum('kgqt,tkh->kgqh', rounded(weight), value_tile) / denominator[..., None]
    live_rows = (query_pos < length)[None, None, :, None]
    return (grouped, key_tile, value_tile, weight, denominator, output, live_rows)

def doc_forward(packed):
    query_doc, key_doc, value_doc, length = packed
    keys_all = padded_states(key_doc)
    values_all = padded_states(value_doc)

    def one_block(block_index):
        state = block_state(query_doc, keys_all, values_all, block_index, length)
        output, live_rows = (state[5], state[6])
        return lax.optimization_barrier(jnp.sum(jnp.where(live_rows, output, 0.0), 2)).reshape(-1)
    pooled = lax.map(one_block, jnp.arange(N_CTX, dtype=jnp.int32))
    return lax.optimization_barrier(jnp.sum(pooled, 0)) / length.astype(jnp.float32)

def doc_backward(packed):
    query_doc, key_doc, value_doc, length, cotangent = packed
    keys_all = padded_states(key_doc)
    values_all = padded_states(value_doc)
    cot_full = cotangent.reshape(HK, HQ // HK, HD)
    cot_round = rounded(cot_full)
    score_scale = HD ** (-0.5)
    tile_rows = (SPAN + 1) * SEQ_DEV

    def one_block(carried, block_index):
        key_grads, value_grads = carried
        grouped, key_tile, value_tile, weight, denominator, output, live_rows = block_state(query_doc, keys_all, values_all, block_index, length)
        attn_prob = jnp.where(live_rows, weight / denominator[..., None], 0.0)
        row_dot = lax.optimization_barrier(jnp.sum(cot_full[:, :, None, :] * output, -1))
        prob_grad = jnp.einsum('kgh,tkh->kgt', cot_round, value_tile)
        score_grad = attn_prob * (prob_grad[:, :, None, :] - row_dot[..., None])
        score_round = rounded(score_grad)
        query_grad = jnp.einsum('kgqt,tkh->qkgh', score_round, key_tile) * score_scale
        key_part = jnp.einsum('kgqt,qkgh->tkh', score_round, grouped) * score_scale
        value_part = jnp.einsum('kgqt,kgh->tkh', rounded(attn_prob), cot_round)
        row_start = block_index * SEQ_DEV
        key_grads = lax.dynamic_update_slice_in_dim(key_grads, lax.dynamic_slice_in_dim(key_grads, row_start, tile_rows, 0) + key_part, row_start, 0)
        value_grads = lax.dynamic_update_slice_in_dim(value_grads, lax.dynamic_slice_in_dim(value_grads, row_start, tile_rows, 0) + value_part, row_start, 0)
        return ((key_grads, value_grads), query_grad.reshape(SEQ_DEV, -1))
    zeros_kv = jnp.zeros(((N_CTX + SPAN) * SEQ_DEV, HK, HD), jnp.float32)
    (key_grads, value_grads), query_grads = lax.scan(one_block, (zeros_kv, zeros_kv), jnp.arange(N_CTX, dtype=jnp.int32))
    key_out = key_grads[SPAN * SEQ_DEV:].reshape(LEN, HK * HD).astype(jnp.bfloat16)
    value_out = value_grads[SPAN * SEQ_DEV:].reshape(LEN, HK * HD).astype(jnp.bfloat16)
    return (query_grads.reshape(LEN, -1).astype(jnp.bfloat16), key_out, value_out)

def reference(query_states, key_states, value_states, lengths, queue_keys, write_pos, teacher):
    pooled = lax.map(doc_forward, (query_states, key_states, value_states, lengths))
    root_mean = jnp.sqrt(lax.optimization_barrier(jnp.mean(pooled * pooled, -1, keepdims=True)) + norm_eps)
    norm_scale = root_mean * pooled.shape[1] ** 0.5
    embedding = pooled / norm_scale
    unit_round = embedding.astype(jnp.bfloat16)
    entry_ids = jnp.arange(QUEUE, dtype=jnp.int32)
    written = entry_ids[:, None] == write_pos[None, :]
    replaced = jnp.dot(written.astype(jnp.bfloat16), unit_round, preferred_element_type=jnp.float32).astype(jnp.bfloat16)
    effective = jnp.where(jnp.any(written, 1)[:, None], replaced, queue_keys)
    logits = jnp.dot(unit_round, effective.T, preferred_element_type=jnp.float32) * inverse_temp
    student = jnp.exp(logits)
    target = jnp.exp(teacher)
    student_total = lax.optimization_barrier(jnp.sum(student, 1))
    target_total = lax.optimization_barrier(jnp.sum(target, 1))
    cross_total = lax.optimization_barrier(jnp.sum(target * (teacher - logits), 1))
    loss_value = jnp.mean(cross_total / target_total - jnp.log(target_total) + jnp.log(student_total))
    grad_logits = loss_scale * (student / student_total[:, None] - target / target_total[:, None]) / DOCS
    unit_grad = jnp.dot(grad_logits.astype(jnp.bfloat16), effective, preferred_element_type=jnp.float32) * inverse_temp
    embedding_grad = (unit_grad - embedding * lax.optimization_barrier(jnp.sum(embedding * unit_grad, -1, keepdims=True))) / norm_scale
    cotangent = embedding_grad / lengths[:, None].astype(jnp.float32)
    grad_query, grad_key, grad_value = lax.map(doc_backward, (query_states, key_states, value_states, lengths, cotangent))
    return (loss_value, embedding, grad_query, grad_key, grad_value)
```

```python
import functools

import jax
import jax.numpy as jnp
from jax import lax
from jax.experimental import pallas as pl
from jax.experimental.pallas import tpu as pltpu
from jax.sharding import PartitionSpec as P

HD = 128
SPAN = 2
HEADS = 16
HALF = 8
DOCS = 8
ENTRIES = 256
EXT = ENTRIES + 128
NZ = 16
PLANE = 32
ROWS = 10

inverse_temp = 10.0
loss_scale = 2.0**24
norm_eps = 1e-06

MESH = pl.DeviceIdType.MESH


def from_behind(x, axis, by):
    devices = lax.axis_size(axis)
    pairs = [(i, i + by) for i in range(devices) if 0 <= i + by < devices]
    return lax.ppermute(x, axis, pairs)


def position():
    ctx = lax.axis_index("ctx")
    grp = lax.axis_index("grp")
    return ctx // 32, (ctx // 2) % NZ, ctx % 2, grp


def device(x_hi, z, core, grp):
    return ((x_hi * NZ + z) * 2 + core, grp)


def plane_peer(step):
    x_hi, z, core, grp = position()
    turn = (step // 4) % 4
    turn = turn + turn // 2 - 2 * (turn // 3)
    px = (x_hi + step // 16) % 2
    pc = (core + step % 2) % 2
    pl_x = (grp // 4 + (step // 2) % 2) % 2
    py = (grp + turn) % 4
    return px, pc, pl_x * 4 + py


def z_offset(step):
    return 8 + ((step + 1) // 2) * (2 * (step % 2) - 1)


def send_plane(src_of, dst, send_sem, recv_sem):
    x_hi, z, core, grp = position()
    mine = x_hi * 16 + core * 8 + grp

    def one(k, carry):
        px, pc, pg = plane_peer(31 - k)
        pltpu.make_async_remote_copy(
            src_ref=src_of(pc, pg),
            dst_ref=dst(mine),
            send_sem=send_sem,
            recv_sem=recv_sem,
            device_id=device(px, z, pc, pg),
            device_id_type=MESH,
        ).start()
        return carry

    lax.fori_loop(0, PLANE - 1, one, 0)


def send_ring(src, dst, send_sem, recv_sem):
    x_hi, z, core, grp = position()

    def one(k, carry):
        pltpu.make_async_remote_copy(
            src_ref=src,
            dst_ref=dst(z),
            send_sem=send_sem,
            recv_sem=recv_sem,
            device_id=device(x_hi, (z + z_offset(k)) % NZ, core, grp),
            device_id_type=MESH,
        ).start()
        return carry

    lax.fori_loop(0, NZ - 1, one, 0)


def core_copy(src, dst, send_sem, recv_sem):
    x_hi, z, core, grp = position()
    return pltpu.make_async_remote_copy(
        src_ref=src,
        dst_ref=dst,
        send_sem=send_sem,
        recv_sem=recv_sem,
        device_id=device(x_hi, z, 1 - core, grp),
        device_id_type=MESH,
    )


def wait_bytes(ref, sem):
    pltpu.make_async_copy(ref, ref, sem).wait()


def sum_slots(ref, count):
    total = ref[0]
    for i in range(1, count):
        total = total + ref[i]
    return total


def two_halves(x):
    high = x.astype(jnp.bfloat16).astype(jnp.float32)
    return jnp.concatenate([high, x - high], 0).astype(jnp.bfloat16)


def queue_kernel(
    pos_ref, len_ref, pooled_ref, queue_ref, teacher_ref,
    emb_ref, cot_ref, loss_ref,
    eff, mix, core_buf, zb, pb, t_out, tp, tz, t_own, t_half, s_out, ep, ez, e_half, half_sum, ring_out,
    t_ring_out, t_full, unit_rows, e_ring_out,
    ready, load_sem, send, recv,
):
    x_hi, z, core, grp = position()
    mine = x_hi * 16 + core * 8 + grp
    barrier = pltpu.get_barrier_semaphore()

    def hello_plane(k, carry):
        px, pc, pg = plane_peer(k + 1)
        pl.semaphore_signal(barrier, inc=1, device_id=device(px, z, pc, pg), device_id_type=MESH)
        return carry

    def hello_ring(k, carry):
        to = (z + NZ - 4 + k + k // 4) % NZ
        pl.semaphore_signal(barrier, inc=1, device_id=device(x_hi, to, core, grp), device_id_type=MESH)
        return carry

    lax.fori_loop(0, 8, hello_ring, 0)
    lax.fori_loop(0, PLANE - 1, hello_plane, 0)
    load = pltpu.make_async_copy(queue_ref, eff.at[pl.ds(0, ENTRIES)], load_sem)
    load.start()
    eff[pl.ds(ENTRIES, 128)] = jnp.zeros((128, 2048), jnp.bfloat16)

    base = ((x_hi * NZ + z) * 2 + core) * (8 * ENTRIES) + grp * ENTRIES
    entry = lax.broadcasted_iota(jnp.int32, (DOCS, ENTRIES), 1) + base
    lane = lax.broadcasted_iota(jnp.int32, (DOCS, 128), 1)
    row = lax.broadcasted_iota(jnp.int32, (DOCS, 128), 0)
    teacher = teacher_ref[...]
    kept = jnp.ones((DOCS, ENTRIES), jnp.float32)
    there = jnp.zeros((DOCS, 128), jnp.float32)
    teacher_at = jnp.zeros((DOCS, 128), jnp.float32)
    for d in range(DOCS):
        hit = (entry == pos_ref[d]).astype(jnp.float32)
        kept = kept - hit
        at = (lane == d).astype(jnp.float32)
        there = there + at * jnp.sum(hit, 1, keepdims=True)
        teacher_at = teacher_at + at * jnp.sum(teacher * hit, 1, keepdims=True)
    target = jnp.where(kept > 0, jnp.exp(teacher), 0.0)
    target_at = jnp.where(there > 0, jnp.exp(teacher_at), 0.0)
    target_sum = jnp.sum(target, 1, keepdims=True) + jnp.sum(target_at, 1, keepdims=True)
    sum_row = jnp.sum(jnp.where(lane == row, target_sum, 0.0), 0, keepdims=True)

    def spread(out, part):
        for h in range(HEADS):
            out[:, h // HALF, h % HALF] = part[:, h * HD : (h + 1) * HD]

    load.wait()
    mixed = jnp.dot(two_halves(target), eff[pl.ds(0, ENTRIES)], preferred_element_type=jnp.float32)
    spread(t_out, mixed[:DOCS] + mixed[DOCS:])
    for c in range(2):
        t_out[:, c, HALF] = target_at
        for d in range(DOCS):
            t_out[d, c, pl.ds(HALF + 1, 1)] = sum_row

    pl.semaphore_wait(barrier, PLANE - 1 + 8)
    for to in (4, NZ - 4):
        pl.semaphore_signal(ready, inc=1, device_id=device(x_hi, (z + to) % NZ, core, grp), device_id_type=MESH)

    send_plane(
        lambda pc, pg: t_out.at[pg, pc, pl.ds(0, ROWS)], lambda me: tp.at[me, pl.ds(0, ROWS)], send.at[0], recv.at[0]
    )
    tp[mine] = t_out[grp, core]

    pair = core_copy(pooled_ref.at[pl.ds((1 - core) * HALF, HALF)], core_buf, send.at[1], recv.at[1])
    pair.start()
    pl.semaphore_wait(ready, 2)
    pair.wait_recv()
    half_sum[...] = pooled_ref[pl.ds(core * HALF, HALF)] + core_buf[...]
    send_ring(half_sum, lambda me: zb.at[me], send.at[2], recv.at[2])
    zb[z] = half_sum[...]

    wait_bytes(tp.at[pl.ds(0, PLANE - 1), pl.ds(0, ROWS)], recv.at[0])
    t_ring_out[...] = sum_slots(tp, PLANE)
    send_ring(t_ring_out.at[pl.ds(0, ROWS)], lambda me: tz.at[me, pl.ds(0, ROWS)], send.at[3], recv.at[3])
    tz[z] = t_ring_out[...]

    wait_bytes(zb.at[pl.ds(0, NZ - 1)], recv.at[2])
    ring_out[...] = sum_slots(zb, NZ)
    send_plane(lambda pc, pg: ring_out, lambda me: pb.at[me], send.at[4], recv.at[4])
    pb[mine] = ring_out[...]

    wait_bytes(tz.at[pl.ds(0, NZ - 1), pl.ds(0, ROWS)], recv.at[3])
    t_own[...] = sum_slots(tz, NZ)
    t_pair = core_copy(t_own.at[pl.ds(0, HALF)], t_half, send.at[5], recv.at[5])
    t_pair.start()

    wait_bytes(pb.at[pl.ds(0, PLANE - 1)], recv.at[4])
    heads = []
    for c in range(2):
        both = pb[pl.ds(c * 8, 8)] + pb[pl.ds(16 + c * 8, 8)]
        unit_rows[:, pl.ds(c * HALF, HALF)] = both
    square = jnp.zeros((DOCS, HD), jnp.float32)
    for h in range(HEADS):
        tile = unit_rows[:, h]
        heads.append(tile)
        square = square + tile * tile
    root_mean = jnp.sqrt(jnp.sum(square, 1, keepdims=True) / 2048.0 + norm_eps)
    norm_scale = root_mean * 2048.0**0.5
    for h in range(HEADS):
        unit = (heads[h] / norm_scale).astype(jnp.bfloat16)
        eff[pl.ds(ENTRIES, 16), h * HD : (h + 1) * HD] = jnp.concatenate([unit, jnp.zeros_like(unit)], 0)
    unit16 = eff[pl.ds(ENTRIES, 16)]
    logits = (
        lax.dot_general(unit16, eff[...], (((1,), (1,)), ((), ())), preferred_element_type=jnp.float32)[:DOCS]
        * inverse_temp
    )
    near, far = logits[:, :ENTRIES], logits[:, ENTRIES:]
    student = jnp.where(kept > 0, jnp.exp(near), 0.0)
    student_at = jnp.where(there > 0, jnp.exp(far), 0.0)
    student_sum = jnp.sum(student, 1, keepdims=True) + jnp.sum(student_at, 1, keepdims=True)
    cross = jnp.sum(target * (teacher - near), 1, keepdims=True) + jnp.sum(
        target_at * (teacher_at - far), 1, keepdims=True
    )
    student_row = jnp.sum(jnp.where(lane == row, student_sum, 0.0), 0, keepdims=True)
    cross_row = jnp.sum(jnp.where(lane == row, cross, 0.0), 0, keepdims=True)
    mixed = jnp.dot(
        two_halves(jnp.concatenate([student, student_at], 1)), eff[...], preferred_element_type=jnp.float32
    )
    spread(s_out, mixed[:DOCS] + mixed[DOCS:])
    extra = jnp.concatenate([student_row, cross_row], 0)
    for c in range(2):
        for d in range(DOCS):
            s_out[d, c, pl.ds(HALF, 2)] = extra
    send_plane(
        lambda pc, pg: s_out.at[pg, pc, pl.ds(0, ROWS)], lambda me: ep.at[me, pl.ds(0, ROWS)], send.at[6], recv.at[6]
    )
    ep[mine] = s_out[grp, core]

    own = unit_rows[grp]
    own_mean = jnp.sqrt(jnp.sum(jnp.sum(own * own, 1, keepdims=True), 0, keepdims=True) / 2048.0 + norm_eps)
    own_scale = own_mean * 2048.0**0.5
    emb = own / own_scale
    emb_ref[...] = emb
    t_pair.wait_recv()
    t_full[pl.ds(core * HALF, HALF)] = t_own[pl.ds(0, HALF)]
    t_full[pl.ds((1 - core) * HALF, HALF)] = t_half[...]
    t_sum = t_full[...]
    lane1 = lax.broadcasted_iota(jnp.int32, (1, 128), 1)
    at_row = t_own[pl.ds(HALF, 1)]
    target_row = t_own[pl.ds(HALF + 1, 1)]
    for d in range(DOCS):
        weight = jnp.sum(jnp.where(lane1 == d, at_row, 0.0), 1, keepdims=True)
        other = unit_rows[d]
        other_mean = jnp.sqrt(jnp.sum(jnp.sum(other * other, 1, keepdims=True), 0, keepdims=True) / 2048.0 + norm_eps)
        other_unit = (other / (other_mean * 2048.0**0.5)).astype(jnp.bfloat16).astype(jnp.float32)
        t_sum = t_sum + weight * other_unit
    target_total = jnp.sum(jnp.where(lane1 == grp, target_row, 0.0), 1, keepdims=True)

    wait_bytes(ep.at[pl.ds(0, PLANE - 1), pl.ds(0, ROWS)], recv.at[6])
    e_ring_out[...] = sum_slots(ep, PLANE)
    send_ring(e_ring_out.at[pl.ds(0, ROWS)], lambda me: ez.at[me, pl.ds(0, ROWS)], send.at[7], recv.at[7])
    ez[z] = e_ring_out[...]
    wait_bytes(ez.at[pl.ds(0, NZ - 1), pl.ds(0, ROWS)], recv.at[7])
    half_sum2 = sum_slots(ez, NZ)
    mix[...] = half_sum2
    e_pair = core_copy(mix.at[pl.ds(0, HALF)], e_half, send.at[8], recv.at[8])
    e_pair.start()
    student_all = mix[pl.ds(HALF, 1)]
    cross_all = mix[pl.ds(HALF + 1, 1)]
    student_total = jnp.sum(jnp.where(lane1 == grp, student_all, 0.0), 1, keepdims=True)
    terms = jnp.where(
        lane1 < DOCS,
        cross_all / jnp.where(lane1 < DOCS, target_row, 1.0)
        - jnp.log(jnp.where(lane1 < DOCS, target_row, 1.0))
        + jnp.log(jnp.where(lane1 < DOCS, student_all, 1.0)),
        0.0,
    )
    loss_ref[...] = jnp.sum(terms, 1, keepdims=True) / DOCS
    e_pair.wait_recv()
    ring_full = t_full
    ring_full[pl.ds(core * HALF, HALF)] = mix[pl.ds(0, HALF)]
    ring_full[pl.ds((1 - core) * HALF, HALF)] = e_half[...]
    unit_grad = (
        inverse_temp * loss_scale / DOCS * (ring_full[...] / student_total - t_sum / target_total)
    )
    inner = jnp.sum(jnp.sum(emb * unit_grad, 1, keepdims=True), 0, keepdims=True)
    cot_ref[...] = (unit_grad - emb * inner) / own_scale / len_ref[0].astype(jnp.float32)

    wait_bytes(tp.at[pl.ds(0, PLANE - 1), pl.ds(0, ROWS)], send.at[0])
    pair.wait_send()
    wait_bytes(zb.at[pl.ds(0, NZ - 1)], send.at[2])
    wait_bytes(tz.at[pl.ds(0, NZ - 1), pl.ds(0, ROWS)], send.at[3])
    wait_bytes(pb.at[pl.ds(0, PLANE - 1)], send.at[4])
    t_pair.wait_send()
    wait_bytes(ep.at[pl.ds(0, PLANE - 1), pl.ds(0, ROWS)], send.at[6])
    wait_bytes(ez.at[pl.ds(0, NZ - 1), pl.ds(0, ROWS)], send.at[7])
    e_pair.wait_send()


def queue_part(pooled, lengths, queue_keys, write_pos, teacher):
    vmem = pl.BlockSpec(memory_space=pltpu.VMEM)
    smem = pl.BlockSpec(memory_space=pltpu.SMEM)
    f32 = lambda *shape: pltpu.VMEM(shape, jnp.float32)
    return pl.pallas_call(
        queue_kernel,
        name="queue_part",
        out_shape=(
            jax.ShapeDtypeStruct((HEADS, HD), jnp.float32),
            jax.ShapeDtypeStruct((HEADS, HD), jnp.float32),
            jax.ShapeDtypeStruct((1, 1), jnp.float32),
        ),
        in_specs=[smem, smem, vmem, pl.BlockSpec(memory_space=pl.ANY), vmem],
        out_specs=(vmem, vmem, vmem),
        scratch_shapes=[
            pltpu.VMEM((EXT, 2048), jnp.bfloat16),
            f32(16, 128),
            f32(HALF, 128),
            f32(NZ, HALF, 128),
            f32(PLANE, HALF, 128),
            f32(DOCS, 2, 16, 128),
            f32(PLANE, 16, 128),
            f32(NZ, 16, 128),
            f32(16, 128),
            f32(HALF, 128),
            f32(DOCS, 2, 16, 128),
            f32(PLANE, 16, 128),
            f32(NZ, 16, 128),
            f32(HALF, 128),
            f32(HALF, 128),
            f32(HALF, 128),
            f32(16, 128),
            f32(HEADS, 128),
            f32(DOCS, HEADS, 128),
            f32(16, 128),
            pltpu.SemaphoreType.REGULAR,
            pltpu.SemaphoreType.DMA,
            pltpu.SemaphoreType.DMA((9,)),
            pltpu.SemaphoreType.DMA((9,)),
        ],
        compiler_params=pltpu.CompilerParams(
            collective_id=0, has_side_effects=True, vmem_limit_bytes=32 * 1024 * 1024
        ),
    )(write_pos, lengths, pooled, queue_keys, teacher)


def shards(query_states, key_states, value_states, lengths, queue_keys, write_pos, teacher):
    docs_here, row_count, width = query_states.shape
    kv_width = key_states.shape[2]
    heads_kv = kv_width // HD
    grouped = query_states.reshape(docs_here, row_count, heads_kv, -1, HD)
    score_scale = HD ** (-0.5)
    ctx_index = lax.axis_index("ctx")
    query_pos = ctx_index * row_count + jnp.arange(row_count, dtype=jnp.int32)
    window_rows = SPAN * row_count
    kv_pair = jnp.stack((key_states, value_states))
    kv_blocks = [kv_pair]
    moving = kv_pair
    for offset in range(SPAN):
        moving = from_behind(moving, "ctx", 1)
        kv_blocks.append(moving)
    weights = []
    denominator = 0.0
    numerator = 0.0
    for offset in range(SPAN + 1):
        key_tile = kv_blocks[offset][0].reshape(docs_here, row_count, heads_kv, HD)
        value_tile = kv_blocks[offset][1].reshape(docs_here, row_count, heads_kv, HD)
        key_pos = (ctx_index - offset) * row_count + jnp.arange(row_count, dtype=jnp.int32)
        visible = (
            (key_pos[None, :] <= query_pos[:, None])
            & (key_pos[None, :] > query_pos[:, None] - window_rows)
            & (key_pos[None, :] >= 0)
        )
        scores = (
            jnp.einsum("dqkgh,dtkh->dkgqt", grouped, key_tile, preferred_element_type=jnp.float32)
            * score_scale
        )
        weight = jnp.where(visible, jnp.exp(scores), 0.0)
        weights.append(weight)
        denominator = denominator + jnp.sum(weight, -1)
        numerator = numerator + jnp.einsum(
            "dkgqt,dtkh->dkgqh",
            weight.astype(jnp.bfloat16),
            value_tile,
            preferred_element_type=jnp.float32,
        )
    output = numerator / denominator[..., None]
    live_rows = (query_pos[None, :] < lengths[:, None])[:, None, None, :, None]
    length_float = lengths[:, None].astype(jnp.float32)
    pooled = jnp.sum(jnp.where(live_rows, output, 0.0), 3).reshape(docs_here, -1) / length_float
    emb, cot, loss = queue_part(
        pooled.reshape(HEADS, HD), lengths, queue_keys, write_pos, teacher
    )
    unit_vec = emb.reshape(docs_here, width)
    loss_value = loss[0, 0]
    cotangent = cot.reshape(docs_here, heads_kv, -1, HD)
    cot_round = cotangent.astype(jnp.bfloat16)
    row_dot = jnp.sum(cotangent[:, :, :, None, :] * output, -1)
    query_grad = 0.0
    tile_grads = []
    for offset in range(SPAN + 1):
        key_tile = kv_blocks[offset][0].reshape(docs_here, row_count, heads_kv, HD)
        value_tile = kv_blocks[offset][1].reshape(docs_here, row_count, heads_kv, HD)
        attn_prob = jnp.where(live_rows, weights[offset] / denominator[..., None], 0.0)
        prob_grad = jnp.einsum(
            "dkgh,dtkh->dkgt", cot_round, value_tile, preferred_element_type=jnp.float32
        )
        score_grad = attn_prob * (prob_grad[:, :, :, None, :] - row_dot[..., None])
        score_round = score_grad.astype(jnp.bfloat16)
        query_grad = query_grad + jnp.einsum(
            "dkgqt,dtkh->dqkgh", score_round, key_tile, preferred_element_type=jnp.float32
        )
        key_part = (
            jnp.einsum(
                "dkgqt,dqkgh->dtkh", score_round, grouped, preferred_element_type=jnp.float32
            )
            * score_scale
        )
        value_part = jnp.einsum(
            "dkgqt,dkgh->dtkh",
            attn_prob.astype(jnp.bfloat16),
            cot_round,
            preferred_element_type=jnp.float32,
        )
        tile_grads.append(
            jnp.stack((key_part, value_part)).reshape(2, docs_here, row_count, kv_width)
        )
    kv_grad = tile_grads[SPAN]
    for offset in range(SPAN - 1, -1, -1):
        kv_grad = from_behind(kv_grad, "ctx", -1) + tile_grads[offset]
    query_out = (query_grad * score_scale).reshape(docs_here, row_count, width).astype(jnp.bfloat16)
    return (
        loss_value,
        unit_vec,
        query_out,
        kv_grad[0].astype(jnp.bfloat16),
        kv_grad[1].astype(jnp.bfloat16),
    )


def solution(mesh):
    placed = (
        P("grp", "ctx", None),
        P("grp", "ctx", None),
        P("grp", "ctx", None),
        P("grp"),
        P(("ctx", "grp"), None),
        P(),
        P(None, ("ctx", "grp")),
    )
    return jax.shard_map(
        shards,
        mesh=mesh,
        in_specs=placed,
        out_specs=(
            P(),
            P("grp", None),
            P("grp", "ctx", None),
            P("grp", "ctx", None),
            P("grp", "ctx", None),
        ),
        check_vma=False,
    )
```

```python
import functools

import jax
import jax.numpy as jnp
from jax import lax
from jax.experimental import pallas as pl
from jax.experimental.pallas import tpu as pltpu
from jax.sharding import PartitionSpec as P

HD = 128
HEADS = 16
GROUPS = 4
BLOCK = 128
HALF = 8
DOCS = 8
ENTRIES = 256
EXT = ENTRIES + 128
NZ = 16
PLANE = 32
ROWS = 10

inverse_temp = 10.0
loss_scale = 2.0**24
norm_eps = 1e-06

MESH = pl.DeviceIdType.MESH


def position():
    ctx = lax.axis_index("ctx")
    grp = lax.axis_index("grp")
    return ctx // 32, (ctx // 2) % NZ, ctx % 2, grp


def device(x_hi, z, core, grp):
    return ((x_hi * NZ + z) * 2 + core, grp)


def plane_peer(step):
    x_hi, z, core, grp = position()
    turn = (step // 4) % 4
    turn = turn + turn // 2 - 2 * (turn // 3)
    px = (x_hi + step // 16) % 2
    pc = (core + step % 2) % 2
    pl_x = (grp // 4 + (step // 2) % 2) % 2
    py = (grp + turn) % 4
    return px, pc, pl_x * 4 + py


def z_offset(step):
    return 8 + ((step + 1) // 2) * (2 * (step % 2) - 1)


def send_plane(src_of, dst, send_sem, recv_sem):
    x_hi, z, core, grp = position()
    mine = x_hi * 16 + core * 8 + grp

    def one(k, carry):
        px, pc, pg = plane_peer(31 - k)
        pltpu.make_async_remote_copy(
            src_ref=src_of(pc, pg),
            dst_ref=dst(mine),
            send_sem=send_sem,
            recv_sem=recv_sem,
            device_id=device(px, z, pc, pg),
            device_id_type=MESH,
        ).start()
        return carry

    lax.fori_loop(0, PLANE - 1, one, 0)


def send_ring(src, dst, send_sem, recv_sem):
    x_hi, z, core, grp = position()

    def one(k, carry):
        pltpu.make_async_remote_copy(
            src_ref=src,
            dst_ref=dst(z),
            send_sem=send_sem,
            recv_sem=recv_sem,
            device_id=device(x_hi, (z + z_offset(k)) % NZ, core, grp),
            device_id_type=MESH,
        ).start()
        return carry

    lax.fori_loop(0, NZ - 1, one, 0)


def core_copy(src, dst, send_sem, recv_sem):
    x_hi, z, core, grp = position()
    return pltpu.make_async_remote_copy(
        src_ref=src,
        dst_ref=dst,
        send_sem=send_sem,
        recv_sem=recv_sem,
        device_id=device(x_hi, z, 1 - core, grp),
        device_id_type=MESH,
    )


def wait_bytes(ref, sem):
    pltpu.make_async_copy(ref, ref, sem).wait()


def sum_slots(ref, count):
    total = ref[0]
    for i in range(1, count):
        total = total + ref[i]
    return total


def two_halves(x):
    high = x.astype(jnp.bfloat16).astype(jnp.float32)
    return jnp.concatenate([high, x - high], 0).astype(jnp.bfloat16)


def whole_kernel(
    pos_ref, len_ref, query_hbm, key_hbm, value_hbm, queue_ref, teacher_hbm,
    loss_ref, emb_ref, dq_ref, dk_ref, dv_ref,
    query, keys, values, teacher_ref, prob, sums, sums_in, dk_out, dk_in, score, pooled_ref,
    eff, mix, core_buf, zb, pb, t_out, tp, tz, t_own, t_half, s_out, ep, ez, e_half, half_sum, ring_out,
    t_ring_out, t_full, unit_rows, e_ring_out,
    ready, load_sem, send, recv, near_send, near_recv,
):
    x_hi, z, core, grp = position()
    mine = x_hi * 16 + core * 8 + grp
    barrier = pltpu.get_barrier_semaphore()

    def hello_plane(k, carry):
        px, pc, pg = plane_peer(k + 1)
        pl.semaphore_signal(barrier, inc=1, device_id=device(px, z, pc, pg), device_id_type=MESH)
        return carry

    def hello_ring(k, carry):
        to = (z + NZ - 4 + k + k // 4) % NZ
        pl.semaphore_signal(barrier, inc=1, device_id=device(x_hi, to, core, grp), device_id_type=MESH)
        return carry

    ctx = (x_hi * NZ + z) * 2 + core
    nearby = {by: ((ctx + 64 + by) % 64, grp) for by in (1, 2, -1, -2)}
    lax.fori_loop(0, 8, hello_ring, 0)
    lax.fori_loop(0, PLANE - 1, hello_plane, 0)
    for to in nearby.values():
        pl.semaphore_signal(barrier, inc=1, device_id=to, device_id_type=MESH)
    own_rows = pl.ds(2 * BLOCK, BLOCK)
    loads = [
        pltpu.make_async_copy(source, goal, load_sem.at[i])
        for i, (source, goal) in enumerate((
            (key_hbm.at[0], keys.at[own_rows]),
            (value_hbm.at[0], values.at[own_rows]),
            (teacher_hbm, teacher_ref),
            (queue_ref, eff.at[pl.ds(0, ENTRIES)]),
            (query_hbm.at[0], query),
        ))
    ]
    for load in loads:
        load.start()
    eff[pl.ds(ENTRIES, 128)] = jnp.zeros((128, 2048), jnp.bfloat16)

    base = ((x_hi * NZ + z) * 2 + core) * (8 * ENTRIES) + grp * ENTRIES
    entry = lax.broadcasted_iota(jnp.int32, (DOCS, ENTRIES), 1) + base
    lane = lax.broadcasted_iota(jnp.int32, (DOCS, 128), 1)
    row = lax.broadcasted_iota(jnp.int32, (DOCS, 128), 0)
    loads[2].wait()
    teacher = teacher_ref[...]
    kept = jnp.ones((DOCS, ENTRIES), jnp.float32)
    there = jnp.zeros((DOCS, 128), jnp.float32)
    teacher_at = jnp.zeros((DOCS, 128), jnp.float32)
    for d in range(DOCS):
        hit = (entry == pos_ref[d]).astype(jnp.float32)
        kept = kept - hit
        at = (lane == d).astype(jnp.float32)
        there = there + at * jnp.sum(hit, 1, keepdims=True)
        teacher_at = teacher_at + at * jnp.sum(teacher * hit, 1, keepdims=True)
    target = jnp.where(kept > 0, jnp.exp(teacher), 0.0)
    target_at = jnp.where(there > 0, jnp.exp(teacher_at), 0.0)
    target_sum = jnp.sum(target, 1, keepdims=True) + jnp.sum(target_at, 1, keepdims=True)
    sum_row = jnp.sum(jnp.where(lane == row, target_sum, 0.0), 0, keepdims=True)

    def spread(out, part):
        for h in range(HEADS):
            out[:, h // HALF, h % HALF] = part[:, h * HD : (h + 1) * HD]

    loads[3].wait()
    mixed = jnp.dot(two_halves(target), eff[pl.ds(0, ENTRIES)], preferred_element_type=jnp.float32)
    spread(t_out, mixed[:DOCS] + mixed[DOCS:])
    for c in range(2):
        t_out[:, c, HALF] = target_at
        for d in range(DOCS):
            t_out[d, c, pl.ds(HALF + 1, 1)] = sum_row

    pl.semaphore_wait(barrier, PLANE - 1 + 8 + 4)
    loads[0].wait()
    loads[1].wait()
    halo = []
    for i, (held, by) in enumerate(((keys, 1), (keys, 2), (values, 1), (values, 2))):
        halo.append(
            pltpu.make_async_remote_copy(
                src_ref=held.at[own_rows],
                dst_ref=held.at[pl.ds((2 - by) * BLOCK, BLOCK)],
                send_sem=near_send.at[i],
                recv_sem=near_recv.at[i],
                device_id=nearby[by],
                device_id_type=MESH,
            )
        )
        halo[-1].start()
    for to in (4, NZ - 4):
        pl.semaphore_signal(ready, inc=1, device_id=device(x_hi, (z + to) % NZ, core, grp), device_id_type=MESH)

    send_plane(
        lambda pc, pg: t_out.at[pg, pc, pl.ds(0, ROWS)], lambda me: tp.at[me, pl.ds(0, ROWS)], send.at[0], recv.at[0]
    )
    tp[mine] = t_out[grp, core]


    loads[4].wait()
    later = lax.broadcasted_iota(jnp.int32, (BLOCK, BLOCK), 1)
    rows = lax.broadcasted_iota(jnp.int32, (BLOCK, BLOCK), 0)
    seen = (
        (later > rows) & (ctx >= 2),
        (later >= 0) & (ctx >= 1),
        later <= rows,
    )

    def stacked(g):
        return jnp.concatenate([query[:, (4 * g + j) * HD : (4 * g + j + 1) * HD] for j in range(4)], 0)

    for block in (2, 1, 0):
        if block < 2:
            halo[1 - block].wait_recv()
        for g in range(GROUPS):
            tile = keys[pl.ds(block * BLOCK, BLOCK), g * HD : (g + 1) * HD]
            scores = lax.dot_general(
                stacked(g), tile, (((1,), (1,)), ((), ())), preferred_element_type=jnp.float32
            )
            weight = jnp.exp(scores * HD ** (-0.5)).reshape(4, BLOCK, BLOCK)
            prob[4 * g : 4 * g + 4, :, block * BLOCK : (block + 1) * BLOCK] = jnp.where(seen[block][None], weight, 0.0)

    length = len_ref[0]
    place = lax.broadcasted_iota(jnp.int32, (BLOCK, 1), 0) + ctx * BLOCK
    live = (place < length).astype(jnp.float32)
    for h in range(HEADS):
        weight = prob[h]
        total = weight[:, :BLOCK] + weight[:, BLOCK : 2 * BLOCK] + weight[:, 2 * BLOCK :]
        part = weight * (live / jnp.sum(total, 1, keepdims=True))
        prob[h] = part
        column = jnp.sum(part, 0, keepdims=True)
        for block in range(3):
            sums[block, pl.ds(h, 1)] = column[:, block * BLOCK : (block + 1) * BLOCK]
    sum_copies = []
    for i, by in enumerate((1, 2)):
        sum_copies.append(
            pltpu.make_async_remote_copy(
                src_ref=sums.at[2 - by],
                dst_ref=sums_in.at[i],
                send_sem=near_send.at[4 + i],
                recv_sem=near_recv.at[4 + i],
                device_id=nearby[-by],
                device_id_type=MESH,
            )
        )
        sum_copies[-1].start()
    halo[2].wait_recv()
    halo[3].wait_recv()
    length_float = length.astype(jnp.float32)
    for g in range(GROUPS):
        column = jnp.concatenate([sums[block, 4 * g : 4 * g + 4] for block in range(3)], 1)
        split = jnp.concatenate([column, jnp.zeros_like(column)], 0)
        out = jnp.dot(two_halves(split), values[:, g * HD : (g + 1) * HD], preferred_element_type=jnp.float32)
        pooled_ref[4 * g : 4 * g + 4] = (out[:4] + out[8:12]) / length_float

    pair = core_copy(pooled_ref.at[pl.ds((1 - core) * HALF, HALF)], core_buf, send.at[1], recv.at[1])
    pair.start()
    pl.semaphore_wait(ready, 2)
    pair.wait_recv()
    half_sum[...] = pooled_ref[pl.ds(core * HALF, HALF)] + core_buf[...]
    send_ring(half_sum, lambda me: zb.at[me], send.at[2], recv.at[2])
    zb[z] = half_sum[...]

    wait_bytes(tp.at[pl.ds(0, PLANE - 1), pl.ds(0, ROWS)], recv.at[0])
    t_ring_out[...] = sum_slots(tp, PLANE)
    send_ring(t_ring_out.at[pl.ds(0, ROWS)], lambda me: tz.at[me, pl.ds(0, ROWS)], send.at[3], recv.at[3])
    tz[z] = t_ring_out[...]

    wait_bytes(zb.at[pl.ds(0, NZ - 1)], recv.at[2])
    ring_out[...] = sum_slots(zb, NZ)
    send_plane(lambda pc, pg: ring_out, lambda me: pb.at[me], send.at[4], recv.at[4])
    pb[mine] = ring_out[...]

    wait_bytes(tz.at[pl.ds(0, NZ - 1), pl.ds(0, ROWS)], recv.at[3])
    t_own[...] = sum_slots(tz, NZ)
    t_pair = core_copy(t_own.at[pl.ds(0, HALF)], t_half, send.at[5], recv.at[5])
    t_pair.start()

    wait_bytes(pb.at[pl.ds(0, PLANE - 1)], recv.at[4])
    heads = []
    for c in range(2):
        both = pb[pl.ds(c * 8, 8)] + pb[pl.ds(16 + c * 8, 8)]
        unit_rows[:, pl.ds(c * HALF, HALF)] = both
    square = jnp.zeros((DOCS, HD), jnp.float32)
    for h in range(HEADS):
        tile = unit_rows[:, h]
        heads.append(tile)
        square = square + tile * tile
    root_mean = jnp.sqrt(jnp.sum(square, 1, keepdims=True) / 2048.0 + norm_eps)
    norm_scale = root_mean * 2048.0**0.5
    for h in range(HEADS):
        unit = (heads[h] / norm_scale).astype(jnp.bfloat16)
        eff[pl.ds(ENTRIES, 16), h * HD : (h + 1) * HD] = jnp.concatenate([unit, jnp.zeros_like(unit)], 0)
    unit16 = eff[pl.ds(ENTRIES, 16)]
    logits = (
        lax.dot_general(unit16, eff[...], (((1,), (1,)), ((), ())), preferred_element_type=jnp.float32)[:DOCS]
        * inverse_temp
    )
    near, far = logits[:, :ENTRIES], logits[:, ENTRIES:]
    student = jnp.where(kept > 0, jnp.exp(near), 0.0)
    student_at = jnp.where(there > 0, jnp.exp(far), 0.0)
    student_sum = jnp.sum(student, 1, keepdims=True) + jnp.sum(student_at, 1, keepdims=True)
    cross = jnp.sum(target * (teacher - near), 1, keepdims=True) + jnp.sum(
        target_at * (teacher_at - far), 1, keepdims=True
    )
    student_row = jnp.sum(jnp.where(lane == row, student_sum, 0.0), 0, keepdims=True)
    cross_row = jnp.sum(jnp.where(lane == row, cross, 0.0), 0, keepdims=True)
    mixed = jnp.dot(
        two_halves(jnp.concatenate([student, student_at], 1)), eff[...], preferred_element_type=jnp.float32
    )
    spread(s_out, mixed[:DOCS] + mixed[DOCS:])
    extra = jnp.concatenate([student_row, cross_row], 0)
    for c in range(2):
        for d in range(DOCS):
            s_out[d, c, pl.ds(HALF, 2)] = extra
    send_plane(
        lambda pc, pg: s_out.at[pg, pc, pl.ds(0, ROWS)], lambda me: ep.at[me, pl.ds(0, ROWS)], send.at[6], recv.at[6]
    )
    ep[mine] = s_out[grp, core]

    own = unit_rows[grp]
    own_mean = jnp.sqrt(jnp.sum(jnp.sum(own * own, 1, keepdims=True), 0, keepdims=True) / 2048.0 + norm_eps)
    own_scale = own_mean * 2048.0**0.5
    emb = own / own_scale
    for h in range(HEADS):
        emb_ref[:, h * HD : (h + 1) * HD] = emb[h : h + 1]
    t_pair.wait_recv()
    t_full[pl.ds(core * HALF, HALF)] = t_own[pl.ds(0, HALF)]
    t_full[pl.ds((1 - core) * HALF, HALF)] = t_half[...]
    t_sum = t_full[...]
    lane1 = lax.broadcasted_iota(jnp.int32, (1, 128), 1)
    at_row = t_own[pl.ds(HALF, 1)]
    target_row = t_own[pl.ds(HALF + 1, 1)]
    for d in range(DOCS):
        weight = jnp.sum(jnp.where(lane1 == d, at_row, 0.0), 1, keepdims=True)
        other = unit_rows[d]
        other_mean = jnp.sqrt(jnp.sum(jnp.sum(other * other, 1, keepdims=True), 0, keepdims=True) / 2048.0 + norm_eps)
        other_unit = (other / (other_mean * 2048.0**0.5)).astype(jnp.bfloat16).astype(jnp.float32)
        t_sum = t_sum + weight * other_unit
    target_total = jnp.sum(jnp.where(lane1 == grp, target_row, 0.0), 1, keepdims=True)

    wait_bytes(ep.at[pl.ds(0, PLANE - 1), pl.ds(0, ROWS)], recv.at[6])
    e_ring_out[...] = sum_slots(ep, PLANE)
    send_ring(e_ring_out.at[pl.ds(0, ROWS)], lambda me: ez.at[me, pl.ds(0, ROWS)], send.at[7], recv.at[7])
    ez[z] = e_ring_out[...]
    wait_bytes(ez.at[pl.ds(0, NZ - 1), pl.ds(0, ROWS)], recv.at[7])
    half_sum2 = sum_slots(ez, NZ)
    mix[...] = half_sum2
    e_pair = core_copy(mix.at[pl.ds(0, HALF)], e_half, send.at[8], recv.at[8])
    e_pair.start()
    student_all = mix[pl.ds(HALF, 1)]
    cross_all = mix[pl.ds(HALF + 1, 1)]
    student_total = jnp.sum(jnp.where(lane1 == grp, student_all, 0.0), 1, keepdims=True)
    terms = jnp.where(
        lane1 < DOCS,
        cross_all / jnp.where(lane1 < DOCS, target_row, 1.0)
        - jnp.log(jnp.where(lane1 < DOCS, target_row, 1.0))
        + jnp.log(jnp.where(lane1 < DOCS, student_all, 1.0)),
        0.0,
    )
    loss_ref[...] = jnp.sum(terms, 1, keepdims=True) / DOCS
    e_pair.wait_recv()
    ring_full = t_full
    ring_full[pl.ds(core * HALF, HALF)] = mix[pl.ds(0, HALF)]
    ring_full[pl.ds((1 - core) * HALF, HALF)] = e_half[...]
    unit_grad = (
        inverse_temp * loss_scale / DOCS * (ring_full[...] / student_total - t_sum / target_total)
    )
    inner = jnp.sum(jnp.sum(emb * unit_grad, 1, keepdims=True), 0, keepdims=True)
    cot = (unit_grad - emb * inner) / own_scale / length_float
    cot_wide = jnp.concatenate([cot] * GROUPS, 1)
    mine_only = lax.broadcasted_iota(jnp.int32, (HEADS, GROUPS * HD), 1) // HD == (
        lax.broadcasted_iota(jnp.int32, (HEADS, GROUPS * HD), 0) // 4
    )
    cot_diag = jnp.where(mine_only, cot_wide, 0.0).astype(jnp.bfloat16)
    prob_grad = lax.dot_general(
        cot_diag, values[...], (((1,), (1,)), ((), ())), preferred_element_type=jnp.float32
    )

    dk_copies = []
    for g in range(GROUPS):
        for j in range(4):
            h = 4 * g + j
            part = prob[h]
            push = part * prob_grad[h : h + 1]
            total = push[:, :BLOCK] + push[:, BLOCK : 2 * BLOCK] + push[:, 2 * BLOCK :]
            score[g, j * BLOCK : (j + 1) * BLOCK] = (push - part * jnp.sum(total, 1, keepdims=True)).astype(
                jnp.bfloat16
            )
        for i, by in enumerate((1, 2)):
            block = 2 - by
            dk_out[i, g] = (
                lax.dot_general(
                    score[g, :, block * BLOCK : (block + 1) * BLOCK],
                    stacked(g),
                    (((0,), (0,)), ((), ())),
                    preferred_element_type=jnp.float32,
                )
                * HD ** (-0.5)
            ).astype(dk_out.dtype)
            copy = pltpu.make_async_remote_copy(
                src_ref=dk_out.at[i, g],
                dst_ref=dk_in.at[i, g],
                send_sem=near_send.at[6 + i],
                recv_sem=near_recv.at[6 + i],
                device_id=nearby[-by],
                device_id_type=MESH,
            )
            copy.start()
    for copy in sum_copies:
        copy.wait_recv()
    sums_all = sums[2] + sums_in[0] + sums_in[1]
    high = sums_all.astype(jnp.bfloat16)
    low = (sums_all - high.astype(jnp.float32)).astype(jnp.bfloat16)
    dv_ref[0] = lax.dot_general(
        jnp.concatenate([high, low], 0),
        jnp.concatenate([cot_diag, cot_diag], 0),
        (((0,), (0,)), ((), ())),
        preferred_element_type=jnp.float32,
    ).astype(jnp.bfloat16)
    dk_own = []
    for g in range(GROUPS):
        dq = jnp.dot(score[g], keys[:, g * HD : (g + 1) * HD], preferred_element_type=jnp.float32) * HD ** (-0.5)
        for j in range(4):
            h = 4 * g + j
            dq_ref[0, :, h * HD : (h + 1) * HD] = dq[j * BLOCK : (j + 1) * BLOCK].astype(jnp.bfloat16)
        dk_own.append(
            lax.dot_general(
                score[g, :, 2 * BLOCK :], stacked(g), (((0,), (0,)), ((), ())), preferred_element_type=jnp.float32
            )
            * HD ** (-0.5)
        )
    for i in range(2):
        wait_bytes(dk_in.at[i], near_recv.at[6 + i])
    for g in range(GROUPS):
        dk_ref[0, :, g * HD : (g + 1) * HD] = (
            dk_own[g] + dk_in[0, g].astype(jnp.float32) + dk_in[1, g].astype(jnp.float32)
        ).astype(jnp.bfloat16)

    for copy in halo + sum_copies:
        copy.wait_send()
    for i in range(2):
        wait_bytes(dk_out.at[i], near_send.at[6 + i])
    wait_bytes(tp.at[pl.ds(0, PLANE - 1), pl.ds(0, ROWS)], send.at[0])
    pair.wait_send()
    wait_bytes(zb.at[pl.ds(0, NZ - 1)], send.at[2])
    wait_bytes(tz.at[pl.ds(0, NZ - 1), pl.ds(0, ROWS)], send.at[3])
    wait_bytes(pb.at[pl.ds(0, PLANE - 1)], send.at[4])
    t_pair.wait_send()
    wait_bytes(ep.at[pl.ds(0, PLANE - 1), pl.ds(0, ROWS)], send.at[6])
    wait_bytes(ez.at[pl.ds(0, NZ - 1), pl.ds(0, ROWS)], send.at[7])
    e_pair.wait_send()


def shards(query_states, key_states, value_states, lengths, queue_keys, write_pos, teacher):
    vmem = pl.BlockSpec(memory_space=pltpu.VMEM)
    smem = pl.BlockSpec(memory_space=pltpu.SMEM)
    anywhere = pl.BlockSpec(memory_space=pl.ANY)

    def f32(*shape):
        return pltpu.VMEM(shape, jnp.float32)

    def b16(*shape):
        return pltpu.VMEM(shape, jnp.bfloat16)

    loss, unit_vec, grad_query, grad_key, grad_value = pl.pallas_call(
        whole_kernel,
        name="whole",
        out_shape=(
            jax.ShapeDtypeStruct((1, 1), jnp.float32),
            jax.ShapeDtypeStruct((1, HEADS * HD), jnp.float32),
            jax.ShapeDtypeStruct(query_states.shape, jnp.bfloat16),
            jax.ShapeDtypeStruct(key_states.shape, jnp.bfloat16),
            jax.ShapeDtypeStruct(value_states.shape, jnp.bfloat16),
        ),
        in_specs=[smem, smem] + [anywhere] * 5,
        out_specs=(vmem,) * 5,
        scratch_shapes=[
            b16(BLOCK, HEADS * HD),
            b16(3 * BLOCK, GROUPS * HD),
            b16(3 * BLOCK, GROUPS * HD),
            f32(DOCS, ENTRIES),
            f32(HEADS, BLOCK, 3 * BLOCK),
            f32(3, HEADS, BLOCK),
            f32(2, HEADS, BLOCK),
            b16(2, GROUPS, BLOCK, HD),
            b16(2, GROUPS, BLOCK, HD),
            b16(GROUPS, 4 * BLOCK, 3 * BLOCK),
            f32(HEADS, HD),
            b16(EXT, 2048),
            f32(16, 128),
            f32(HALF, 128),
            f32(NZ, HALF, 128),
            f32(PLANE, HALF, 128),
            f32(DOCS, 2, 16, 128),
            f32(PLANE, 16, 128),
            f32(NZ, 16, 128),
            f32(16, 128),
            f32(HALF, 128),
            f32(DOCS, 2, 16, 128),
            f32(PLANE, 16, 128),
            f32(NZ, 16, 128),
            f32(HALF, 128),
            f32(HALF, 128),
            f32(HALF, 128),
            f32(16, 128),
            f32(HEADS, 128),
            f32(DOCS, HEADS, 128),
            f32(16, 128),
            pltpu.SemaphoreType.REGULAR,
            pltpu.SemaphoreType.DMA((5,)),
            pltpu.SemaphoreType.DMA((9,)),
            pltpu.SemaphoreType.DMA((9,)),
            pltpu.SemaphoreType.DMA((8,)),
            pltpu.SemaphoreType.DMA((8,)),
        ],
        compiler_params=pltpu.CompilerParams(
            collective_id=0, has_side_effects=True, vmem_limit_bytes=40 * 1024 * 1024
        ),
    )(write_pos, lengths, query_states, key_states, value_states, queue_keys, teacher)
    return loss[0, 0], unit_vec, grad_query, grad_key, grad_value


def solution(mesh):
    placed = (
        P("grp", "ctx", None),
        P("grp", "ctx", None),
        P("grp", "ctx", None),
        P("grp"),
        P(("ctx", "grp"), None),
        P(),
        P(None, ("ctx", "grp")),
    )
    return jax.shard_map(
        shards,
        mesh=mesh,
        in_specs=placed,
        out_specs=(
            P(),
            P("grp", None),
            P("grp", "ctx", None),
            P("grp", "ctx", None),
            P("grp", "ctx", None),
        ),
        check_vma=False,
    )
```

```python
import functools

import jax
import jax.numpy as jnp
from jax import lax
from jax.experimental import pallas as pl
from jax.experimental.pallas import tpu as pltpu
from jax.sharding import PartitionSpec as P

HD = 128
HEADS = 16
GROUPS = 2
BLOCK = 128
KV = GROUPS * HD
CHIPS = 32
HALF = 8
WIDE = HALF * HD
DOCS = 8
ENTRIES = 256
EXT = ENTRIES + 128
NZ = 16
PLANE = 32
T_ROWS = 10
ROWS = 11

inverse_temp = 10.0
loss_scale = 2.0**24
norm_eps = 1e-06

MESH = pl.DeviceIdType.MESH


def position():
    ctx = lax.axis_index("ctx")
    grp = lax.axis_index("grp")
    return ctx // 32, (ctx // 2) % NZ, ctx % 2, grp


def device(x_hi, z, core, grp):
    return ((x_hi * NZ + z) * 2 + core, grp)


def shifted(dx=0, dy=0, dz=0, dc=0):
    x_hi, z, core, grp = position()
    x = (2 * x_hi + grp // 4 + dx) % 4
    return device(x // 2, (z + dz) % NZ, (core + dc) % 2, (x % 2) * 4 + (grp + dy) % 4)


def plane_peer(step):
    x_hi, z, core, grp = position()
    turn = (step // 4) % 4
    turn = turn + turn // 2 - 2 * (turn // 3)
    px = (x_hi + step // 16) % 2
    pc = (core + step % 2) % 2
    pl_x = (grp // 4 + (step // 2) % 2) % 2
    py = (grp + turn) % 4
    return px, pc, pl_x * 4 + py


def z_offset(step):
    return 8 + ((step + 1) // 2) * (2 * (step % 2) - 1)


def send_plane(src_of, dst, send_sem, recv_sem):
    x_hi, z, core, grp = position()
    mine = x_hi * 16 + core * 8 + grp

    def one(k, carry):
        px, pc, pg = plane_peer(31 - k)
        pltpu.make_async_remote_copy(
            src_ref=src_of(pc, pg),
            dst_ref=dst(mine),
            send_sem=send_sem,
            recv_sem=recv_sem,
            device_id=device(px, z, pc, pg),
            device_id_type=MESH,
        ).start()
        return carry

    lax.fori_loop(0, PLANE - 1, one, 0)


def send_ring(src, dst, send_sem, recv_sem):
    x_hi, z, core, grp = position()

    def one(k, carry):
        pltpu.make_async_remote_copy(
            src_ref=src,
            dst_ref=dst(z),
            send_sem=send_sem,
            recv_sem=recv_sem,
            device_id=device(x_hi, (z + z_offset(k)) % NZ, core, grp),
            device_id_type=MESH,
        ).start()
        return carry

    lax.fori_loop(0, NZ - 1, one, 0)


def wait_bytes(ref, sem):
    pltpu.make_async_copy(ref, ref, sem).wait()


def sum_slots(ref, count):
    total = ref[0]
    for i in range(1, count):
        total = total + ref[i]
    return total


def two_halves(x):
    high = x.astype(jnp.bfloat16).astype(jnp.float32)
    return jnp.concatenate([high, x - high], 0).astype(jnp.bfloat16)


def whole_kernel(
    pos_ref, len_ref, query_hbm, key_hbm, value_hbm, queue_ref, teacher_hbm,
    loss_ref, emb_ref, dq_ref, dk_ref, dv_ref,
    query_out, key_out, value_out, query, keys, values, teacher_ref, prob, sums, sums_in, score,
    dk_out, dk_in, dk_chip, dk_part, dv_chip, dv_part, dq_chip, dq_part,
    eff, mix, zb, pb, t_out, tp, tz, t_own, t_half, s_out, ep, ez, half_sum, ring_out,
    t_ring_out, t_full, unit_rows, e_ring_out,
    ready, load_sem, send, recv, near_send, near_recv,
):
    x_hi, z, core, grp = position()
    mine = x_hi * 16 + core * 8 + grp
    ctx = (x_hi * NZ + z) * 2 + core
    chip = x_hi * NZ + z
    twin = (chip * 2 + 1 - core, grp)

    def beside(by, which):
        return ((chip + CHIPS + by) % CHIPS * 2 + which, grp)

    barrier = pltpu.get_barrier_semaphore()
    first = [shifted(dx=dx, dy=dy) for dx in (1, 3) for dy in (1, 3)]
    first += [shifted(dz=2), shifted(dz=NZ - 2), shifted(dx=2), shifted(dy=2)]
    first += [beside(by, which) for by in (1, -1) for which in (0, 1)]
    first += [shifted(dz=1), shifted(dz=NZ - 1), shifted(dx=1), shifted(dx=3), shifted(dy=1), shifted(dy=3), twin]
    for to in first:
        pl.semaphore_signal(barrier, inc=1, device_id=to, device_id_type=MESH)

    loads = []
    for i, (source, goal) in enumerate((
        (key_hbm.at[0, :, pl.ds(0, KV)], key_out.at[0]),
        (key_hbm.at[0, :, pl.ds(KV, KV)], key_out.at[1]),
        (query_hbm.at[0, :, pl.ds(0, WIDE)], query_out.at[0]),
        (query_hbm.at[0, :, pl.ds(WIDE, WIDE)], query_out.at[1]),
        (value_hbm.at[0, :, pl.ds(0, KV)], value_out.at[0]),
        (value_hbm.at[0, :, pl.ds(KV, KV)], value_out.at[1]),
        (teacher_hbm, teacher_ref),
        (queue_ref, eff.at[pl.ds(0, ENTRIES)]),
        (key_hbm.at[0, :, pl.ds(pl.multiple_of(core * KV, KV), KV)], keys.at[2 + core]),
        (query_hbm.at[0, :, pl.ds(pl.multiple_of(core * WIDE, WIDE), WIDE)], query.at[core]),
        (value_hbm.at[0, :, pl.ds(pl.multiple_of(core * KV, KV), KV)], values.at[2 + core]),
    )):
        loads.append(pltpu.make_async_copy(source, goal, load_sem.at[i]))
        loads[-1].start()
    eff[pl.ds(ENTRIES, 128)] = jnp.zeros((128, 2048), jnp.bfloat16)

    for i in range(6):
        loads[i].wait()
    pl.semaphore_wait(barrier, len(first))

    def start(source, goal, which, to):
        copy = pltpu.make_async_remote_copy(
            src_ref=source,
            dst_ref=goal,
            send_sem=near_send.at[which],
            recv_sem=near_recv.at[which],
            device_id=to,
            device_id_type=MESH,
        )
        copy.start()
        return copy

    def to_next(source, goal, which):
        for half in range(2):
            pltpu.make_async_remote_copy(
                src_ref=source.at[half],
                dst_ref=goal.at[core],
                send_sem=near_send.at[which + half],
                recv_sem=near_recv.at[which + core],
                device_id=beside(1, half),
                device_id_type=MESH,
            ).start()

    to_next(key_out, keys, 0)
    start(key_out.at[1 - core], keys.at[2 + core], 2, twin)
    start(query_out.at[1 - core], query.at[core], 3, twin)
    start(value_out.at[1 - core], values.at[2 + core], 6, twin)
    to_next(value_out, values, 4)
    for to in (shifted(dz=2), shifted(dz=NZ - 2), shifted(dx=2), shifted(dy=2), twin):
        pl.semaphore_signal(ready.at[0], inc=1, device_id=to, device_id_type=MESH)

    base = (ctx * 8 + grp) * ENTRIES
    entry = lax.broadcasted_iota(jnp.int32, (DOCS, ENTRIES), 1) + base
    lane = lax.broadcasted_iota(jnp.int32, (DOCS, 128), 1)
    row = lax.broadcasted_iota(jnp.int32, (DOCS, 128), 0)
    loads[6].wait()
    teacher = teacher_ref[...]
    kept = jnp.ones((DOCS, ENTRIES), jnp.float32)
    there = jnp.zeros((DOCS, 128), jnp.float32)
    teacher_at = jnp.zeros((DOCS, 128), jnp.float32)
    for d in range(DOCS):
        hit = (entry == pos_ref[d]).astype(jnp.float32)
        kept = kept - hit
        at = (lane == d).astype(jnp.float32)
        there = there + at * jnp.sum(hit, 1, keepdims=True)
        teacher_at = teacher_at + at * jnp.sum(teacher * hit, 1, keepdims=True)
    target = jnp.where(kept > 0, jnp.exp(teacher), 0.0)
    target_at = jnp.where(there > 0, jnp.exp(teacher_at), 0.0)
    target_sum = jnp.sum(target, 1, keepdims=True) + jnp.sum(target_at, 1, keepdims=True)
    sum_row = jnp.sum(jnp.where(lane == row, target_sum, 0.0), 0, keepdims=True)

    def spread(out, part):
        for h in range(HEADS):
            out[:, h // HALF, h % HALF] = part[:, h * HD : (h + 1) * HD]

    loads[7].wait()
    mixed = jnp.dot(two_halves(target), eff[pl.ds(0, ENTRIES)], preferred_element_type=jnp.float32)
    spread(t_out, mixed[:DOCS] + mixed[DOCS:])
    for c in range(2):
        t_out[:, c, HALF] = target_at
        for d in range(DOCS):
            t_out[d, c, pl.ds(HALF + 1, 1)] = sum_row

    pl.semaphore_wait(ready.at[0], 5)
    pl.semaphore_signal(ready.at[1], inc=1, device_id=twin, device_id_type=MESH)
    for to in (4, NZ - 4):
        pl.semaphore_signal(ready.at[2], inc=1, device_id=shifted(dz=to), device_id_type=MESH)

    later = lax.broadcasted_iota(jnp.int32, (BLOCK, BLOCK), 1)
    rows = lax.broadcasted_iota(jnp.int32, (BLOCK, BLOCK), 0)
    inside = (later > rows, None, later <= rows)

    def stacked(r, g):
        return jnp.concatenate([query[r, :, (4 * g + j) * HD : (4 * g + j + 1) * HD] for j in range(4)], 0)

    def weigh(r, s):
        for g in range(GROUPS):
            tile = keys[r + s, :, g * HD : (g + 1) * HD]
            scores = lax.dot_general(
                stacked(r, g), tile, (((1,), (1,)), ((), ())), preferred_element_type=jnp.float32
            )
            weight = jnp.exp(scores * HD ** (-0.5)).reshape(4, BLOCK, BLOCK)
            seen = inside[s]
            if r + s < 2:
                before = jnp.broadcast_to(chip >= 1, (BLOCK, BLOCK))
                seen = before if seen is None else seen & before
            if seen is not None:
                weight = jnp.where(seen[None], weight, 0.0)
            prob[r, 4 * g : 4 * g + 4, :, s * BLOCK : (s + 1) * BLOCK] = weight

    def arrived(ref, which):
        wait_bytes(ref, near_recv.at[which])

    for i in (8, 9, 10):
        loads[i].wait()
    arrived(key_out.at[0], 2)
    arrived(query_out.at[0], 3)
    weigh(0, 2)
    weigh(1, 1)
    weigh(1, 2)
    arrived(key_out.at[0], 0)
    arrived(key_out.at[0], 1)
    weigh(0, 0)
    weigh(0, 1)
    weigh(1, 0)

    length = len_ref[0]
    column = []
    for r in range(2):
        place = lax.broadcasted_iota(jnp.int32, (BLOCK, 1), 0) + (chip * 2 + r) * BLOCK
        live = (place < length).astype(jnp.float32)
        for h in range(HALF):
            weight = prob[r, h]
            total = weight[:, :BLOCK] + weight[:, BLOCK : 2 * BLOCK] + weight[:, 2 * BLOCK :]
            part = weight * (live / jnp.sum(total, 1, keepdims=True))
            prob[r, h] = part
            column.append(jnp.sum(part, 0, keepdims=True))
    for block in range(4):
        parts = []
        for r in range(2):
            s = block - r
            if 0 <= s < 3:
                parts.append(
                    jnp.concatenate([column[r * HALF + h][:, s * BLOCK : (s + 1) * BLOCK] for h in range(HALF)], 0)
                )
        sums[block] = parts[0] if len(parts) == 1 else parts[0] + parts[1]
    start(sums.at[pl.ds(0, 2)], sums_in, 7, beside(-1, core))

    pl.semaphore_wait(ready.at[1], 1)
    send_plane(
        lambda pc, pg: t_out.at[pg, pc, pl.ds(0, T_ROWS)],
        lambda me: tp.at[me, pl.ds(0, T_ROWS)],
        send.at[0],
        recv.at[0],
    )
    tp[mine] = t_out[grp, core]

    arrived(value_out.at[0], 6)
    arrived(sums_in, 7)
    length_float = length.astype(jnp.float32)
    sums_all = sums[pl.ds(2, 2)] + sums_in[...]
    for g in range(GROUPS):
        both = jnp.concatenate([sums_all[b, 4 * g : 4 * g + 4] for b in range(2)], 1)
        split = jnp.concatenate([both, jnp.zeros_like(both)], 0)
        tile = values[pl.ds(2, 2), :, g * HD : (g + 1) * HD].reshape(2 * BLOCK, HD)
        out = jnp.dot(two_halves(split), tile, preferred_element_type=jnp.float32)
        half_sum[4 * g : 4 * g + 4] = (out[:4] + out[8:12]) / length_float

    pl.semaphore_wait(ready.at[2], 2)
    send_ring(half_sum, lambda me: zb.at[me], send.at[2], recv.at[2])
    zb[z] = half_sum[...]

    wait_bytes(tp.at[pl.ds(0, PLANE - 1), pl.ds(0, T_ROWS)], recv.at[0])
    t_ring_out[...] = sum_slots(tp, PLANE)
    send_ring(t_ring_out.at[pl.ds(0, T_ROWS)], lambda me: tz.at[me, pl.ds(0, T_ROWS)], send.at[3], recv.at[3])
    tz[z] = t_ring_out[...]

    wait_bytes(zb.at[pl.ds(0, NZ - 1)], recv.at[2])
    ring_out[...] = sum_slots(zb, NZ)
    send_plane(lambda pc, pg: ring_out, lambda me: pb.at[me], send.at[4], recv.at[4])
    pb[mine] = ring_out[...]

    wait_bytes(tz.at[pl.ds(0, NZ - 1), pl.ds(0, T_ROWS)], recv.at[3])
    t_own[...] = sum_slots(tz, NZ)
    t_pair = pltpu.make_async_remote_copy(
        src_ref=t_own.at[pl.ds(0, HALF)],
        dst_ref=t_half,
        send_sem=send.at[5],
        recv_sem=recv.at[5],
        device_id=twin,
        device_id_type=MESH,
    )
    t_pair.start()

    wait_bytes(pb.at[pl.ds(0, PLANE - 1)], recv.at[4])
    heads = []
    for c in range(2):
        both = pb[pl.ds(c * 8, 8)] + pb[pl.ds(16 + c * 8, 8)]
        unit_rows[:, pl.ds(c * HALF, HALF)] = both
    square = jnp.zeros((DOCS, HD), jnp.float32)
    for h in range(HEADS):
        tile = unit_rows[:, h]
        heads.append(tile)
        square = square + tile * tile
    root_mean = jnp.sqrt(jnp.sum(square, 1, keepdims=True) / 2048.0 + norm_eps)
    norm_scale = root_mean * 2048.0**0.5
    for h in range(HEADS):
        unit = (heads[h] / norm_scale).astype(jnp.bfloat16)
        eff[pl.ds(ENTRIES, 16), h * HD : (h + 1) * HD] = jnp.concatenate([unit, jnp.zeros_like(unit)], 0)
    unit16 = eff[pl.ds(ENTRIES, 16)]
    logits = (
        lax.dot_general(unit16, eff[...], (((1,), (1,)), ((), ())), preferred_element_type=jnp.float32)[:DOCS]
        * inverse_temp
    )
    near, far = logits[:, :ENTRIES], logits[:, ENTRIES:]
    student = jnp.where(kept > 0, jnp.exp(near), 0.0)
    student_at = jnp.where(there > 0, jnp.exp(far), 0.0)
    student_sum = jnp.sum(student, 1, keepdims=True) + jnp.sum(student_at, 1, keepdims=True)
    cross = jnp.sum(target * (teacher - near), 1, keepdims=True) + jnp.sum(
        target_at * (teacher_at - far), 1, keepdims=True
    )
    student_row = jnp.sum(jnp.where(lane == row, student_sum, 0.0), 0, keepdims=True)
    cross_row = jnp.sum(jnp.where(lane == row, cross, 0.0), 0, keepdims=True)
    inner = jnp.sum(student * near, 1, keepdims=True) + jnp.sum(student_at * far, 1, keepdims=True)
    inner_row = jnp.sum(jnp.where(lane == row, inner, 0.0), 0, keepdims=True)
    mixed = jnp.dot(
        two_halves(jnp.concatenate([student, student_at], 1)), eff[...], preferred_element_type=jnp.float32
    )
    spread(s_out, mixed[:DOCS] + mixed[DOCS:])
    extra = jnp.concatenate([student_row, cross_row, inner_row], 0)
    for c in range(2):
        for d in range(DOCS):
            s_out[d, c, pl.ds(HALF, 3)] = extra
    send_plane(
        lambda pc, pg: s_out.at[pg, pc, pl.ds(0, ROWS)], lambda me: ep.at[me, pl.ds(0, ROWS)], send.at[6], recv.at[6]
    )
    ep[mine] = s_out[grp, core]

    own = unit_rows[grp]
    own_mean = jnp.sqrt(jnp.sum(jnp.sum(own * own, 1, keepdims=True), 0, keepdims=True) / 2048.0 + norm_eps)
    own_scale = own_mean * 2048.0**0.5
    emb = own / own_scale
    for h in range(HEADS):
        emb_ref[:, h * HD : (h + 1) * HD] = emb[h : h + 1]
    emb_half = unit_rows[grp, pl.ds(pl.multiple_of(core * HALF, HALF), HALF)] / own_scale
    t_pair.wait_recv()
    t_full[pl.ds(pl.multiple_of(core * HALF, HALF), HALF)] = t_own[pl.ds(0, HALF)]
    t_full[pl.ds(pl.multiple_of((1 - core) * HALF, HALF), HALF)] = t_half[...]
    t_sum = t_full[...]
    lane1 = lax.broadcasted_iota(jnp.int32, (1, 128), 1)
    at_row = t_own[pl.ds(HALF, 1)]
    target_row = t_own[pl.ds(HALF + 1, 1)]
    for d in range(DOCS):
        weight = jnp.sum(jnp.where(lane1 == d, at_row, 0.0), 1, keepdims=True)
        other = unit_rows[d]
        other_mean = jnp.sqrt(jnp.sum(jnp.sum(other * other, 1, keepdims=True), 0, keepdims=True) / 2048.0 + norm_eps)
        other_unit = (other / (other_mean * 2048.0**0.5)).astype(jnp.bfloat16).astype(jnp.float32)
        t_sum = t_sum + weight * other_unit
    target_total = jnp.sum(jnp.where(lane1 == grp, target_row, 0.0), 1, keepdims=True)
    unit_own = emb.astype(jnp.bfloat16).astype(jnp.float32)
    t_inner = jnp.sum(jnp.sum(unit_own * t_sum, 1, keepdims=True), 0, keepdims=True) / target_total
    t_full[...] = t_sum
    t_mean = t_full[pl.ds(pl.multiple_of(core * HALF, HALF), HALF)] / target_total
    mine_only = lax.broadcasted_iota(jnp.int32, (HALF, KV), 1) // HD == (
        lax.broadcasted_iota(jnp.int32, (HALF, KV), 0) // 4
    )
    arrived(value_out.at[0], 4)
    arrived(value_out.at[0], 5)

    wait_bytes(ep.at[pl.ds(0, PLANE - 1), pl.ds(0, ROWS)], recv.at[6])
    e_ring_out[...] = sum_slots(ep, PLANE)
    send_ring(e_ring_out.at[pl.ds(0, ROWS)], lambda me: ez.at[me, pl.ds(0, ROWS)], send.at[7], recv.at[7])
    ez[z] = e_ring_out[...]
    wait_bytes(ez.at[pl.ds(0, NZ - 1), pl.ds(0, ROWS)], recv.at[7])
    mix[...] = sum_slots(ez, NZ)
    student_all = mix[pl.ds(HALF, 1)]
    cross_all = mix[pl.ds(HALF + 1, 1)]
    student_total = jnp.sum(jnp.where(lane1 == grp, student_all, 0.0), 1, keepdims=True)
    s_inner = jnp.sum(jnp.where(lane1 == grp, mix[pl.ds(HALF + 2, 1)], 0.0), 1, keepdims=True) / (
        inverse_temp * student_total
    )
    factor = inverse_temp * loss_scale / DOCS
    unit_grad = factor * (mix[pl.ds(0, HALF)] / student_total - t_mean)
    cot = (unit_grad - emb_half * (factor * (s_inner - t_inner))) / own_scale / length_float
    cot_diag = jnp.where(mine_only, jnp.concatenate([cot] * GROUPS, 1), 0.0)
    cot_diag = jnp.concatenate([cot_diag, jnp.zeros_like(cot_diag)], 0).astype(jnp.bfloat16)
    prob_grad = lax.dot_general(
        cot_diag, values[...].reshape(4 * BLOCK, KV), (((1,), (1,)), ((), ())), preferred_element_type=jnp.float32
    )

    def scored(r):
        for h in range(HALF):
            part = prob[r, h]
            push = part * prob_grad[h : h + 1, r * BLOCK : (r + 3) * BLOCK]
            total = push[:, :BLOCK] + push[:, BLOCK : 2 * BLOCK] + push[:, 2 * BLOCK :]
            score[r, h // 4, (h % 4) * BLOCK : (h % 4 + 1) * BLOCK] = (
                push - part * jnp.sum(total, 1, keepdims=True)
            ).astype(jnp.bfloat16)

    def key_grad(block, g):
        total = None
        for r in range(2):
            s = block - r
            if 0 <= s < 3:
                one = lax.dot_general(
                    score[r, g, :, s * BLOCK : (s + 1) * BLOCK],
                    stacked(r, g),
                    (((0,), (0,)), ((), ())),
                    preferred_element_type=jnp.float32,
                )
                total = one if total is None else total + one
        return total * HD ** (-0.5)

    def send_back(block):
        for g in range(GROUPS):
            dk_out[block, :, g * HD : (g + 1) * HD] = key_grad(block, g).astype(jnp.bfloat16)
        pltpu.make_async_remote_copy(
            src_ref=dk_out.at[block],
            dst_ref=dk_in.at[core],
            send_sem=near_send.at[8 + block],
            recv_sem=near_recv.at[8 + core],
            device_id=beside(-1, block),
            device_id_type=MESH,
        ).start()

    scored(0)
    send_back(0)
    scored(1)
    send_back(1)
    for r in range(2):
        for g in range(GROUPS):
            tile = keys[pl.ds(r, 3), :, g * HD : (g + 1) * HD].reshape(3 * BLOCK, HD)
            dq = jnp.dot(score[r, g], tile, preferred_element_type=jnp.float32) * HD ** (-0.5)
            for j in range(4):
                h = 4 * g + j
                dq_chip[r, :, h * HD : (h + 1) * HD] = dq[j * BLOCK : (j + 1) * BLOCK].astype(jnp.bfloat16)
    start(dq_chip.at[1 - core], dq_part.at[core], 10, twin)
    for block in range(2):
        for g in range(GROUPS):
            dk_chip[block, :, g * HD : (g + 1) * HD] = key_grad(2 + block, g)
    start(dk_chip.at[1 - core], dk_part.at[core], 11, twin)
    for block in range(2):
        high = sums_all[block].astype(jnp.bfloat16).astype(jnp.float32)
        dv_chip[block] = lax.dot_general(
            jnp.concatenate([high, sums_all[block] - high], 0).astype(jnp.bfloat16),
            jnp.concatenate([cot_diag[:HALF], cot_diag[:HALF]], 0),
            (((0,), (0,)), ((), ())),
            preferred_element_type=jnp.float32,
        ).astype(jnp.bfloat16)
    start(dv_chip.at[1 - core], dv_part.at[core], 12, twin)
    dq_part[core] = dq_chip[core]
    dk_part[core] = dk_chip[core]
    dv_part[core] = dv_chip[core]
    terms = jnp.where(
        lane1 < DOCS,
        cross_all / jnp.where(lane1 < DOCS, target_row, 1.0)
        - jnp.log(jnp.where(lane1 < DOCS, target_row, 1.0))
        + jnp.log(jnp.where(lane1 < DOCS, student_all, 1.0)),
        0.0,
    )
    loss_ref[...] = jnp.sum(terms, 1, keepdims=True) / DOCS
    arrived(dq_chip.at[0], 10)
    for half in range(2):
        dq_ref[0, :, half * WIDE : (half + 1) * WIDE] = dq_part[half]
    arrived(dv_chip.at[0], 12)
    for half in range(2):
        dv_ref[0, :, half * KV : (half + 1) * KV] = dv_part[half]
    arrived(dk_chip.at[0], 11)
    for half in range(2):
        arrived(dk_out.at[0], 8 + half)
        dk_ref[0, :, half * KV : (half + 1) * KV] = (dk_part[half] + dk_in[half].astype(jnp.float32)).astype(
            jnp.bfloat16
        )

    for ref, which in (
        (key_out.at[0], 0), (key_out.at[0], 1), (key_out.at[0], 2), (query_out.at[0], 3), (value_out.at[0], 4),
        (value_out.at[0], 5), (value_out.at[0], 6), (sums_in, 7), (dk_out.at[0], 8), (dk_out.at[0], 9),
        (dq_chip.at[0], 10), (dk_chip.at[0], 11), (dv_chip.at[0], 12),
    ):
        wait_bytes(ref, near_send.at[which])
    wait_bytes(tp.at[pl.ds(0, PLANE - 1), pl.ds(0, T_ROWS)], send.at[0])
    wait_bytes(zb.at[pl.ds(0, NZ - 1)], send.at[2])
    wait_bytes(tz.at[pl.ds(0, NZ - 1), pl.ds(0, T_ROWS)], send.at[3])
    wait_bytes(pb.at[pl.ds(0, PLANE - 1)], send.at[4])
    t_pair.wait_send()
    wait_bytes(ep.at[pl.ds(0, PLANE - 1), pl.ds(0, ROWS)], send.at[6])
    wait_bytes(ez.at[pl.ds(0, NZ - 1), pl.ds(0, ROWS)], send.at[7])


def shards(query_states, key_states, value_states, lengths, queue_keys, write_pos, teacher):
    vmem = pl.BlockSpec(memory_space=pltpu.VMEM)
    smem = pl.BlockSpec(memory_space=pltpu.SMEM)
    anywhere = pl.BlockSpec(memory_space=pl.ANY)

    def f32(*shape):
        return pltpu.VMEM(shape, jnp.float32)

    def b16(*shape):
        return pltpu.VMEM(shape, jnp.bfloat16)

    loss, unit_vec, grad_query, grad_key, grad_value = pl.pallas_call(
        whole_kernel,
        name="whole",
        out_shape=(
            jax.ShapeDtypeStruct((1, 1), jnp.float32),
            jax.ShapeDtypeStruct((1, HEADS * HD), jnp.float32),
            jax.ShapeDtypeStruct(query_states.shape, jnp.bfloat16),
            jax.ShapeDtypeStruct(key_states.shape, jnp.bfloat16),
            jax.ShapeDtypeStruct(value_states.shape, jnp.bfloat16),
        ),
        in_specs=[smem, smem] + [anywhere] * 5,
        out_specs=(vmem,) * 5,
        scratch_shapes=[
            b16(2, BLOCK, WIDE),
            b16(2, BLOCK, KV),
            b16(2, BLOCK, KV),
            b16(2, BLOCK, WIDE),
            b16(4, BLOCK, KV),
            b16(4, BLOCK, KV),
            f32(DOCS, ENTRIES),
            f32(2, HALF, BLOCK, 3 * BLOCK),
            f32(4, HALF, BLOCK),
            f32(2, HALF, BLOCK),
            b16(2, GROUPS, 4 * BLOCK, 3 * BLOCK),
            b16(2, BLOCK, KV),
            b16(2, BLOCK, KV),
            f32(2, BLOCK, KV),
            f32(2, BLOCK, KV),
            b16(2, BLOCK, KV),
            b16(2, BLOCK, KV),
            b16(2, BLOCK, WIDE),
            b16(2, BLOCK, WIDE),
            b16(EXT, 2048),
            f32(16, 128),
            f32(NZ, HALF, 128),
            f32(PLANE, HALF, 128),
            f32(DOCS, 2, 16, 128),
            f32(PLANE, 16, 128),
            f32(NZ, 16, 128),
            f32(16, 128),
            f32(HALF, 128),
            f32(DOCS, 2, 16, 128),
            f32(PLANE, 16, 128),
            f32(NZ, 16, 128),
            f32(HALF, 128),
            f32(HALF, 128),
            f32(16, 128),
            f32(HEADS, 128),
            f32(DOCS, HEADS, 128),
            f32(16, 128),
            pltpu.SemaphoreType.REGULAR((3,)),
            pltpu.SemaphoreType.DMA((11,)),
            pltpu.SemaphoreType.DMA((8,)),
            pltpu.SemaphoreType.DMA((8,)),
            pltpu.SemaphoreType.DMA((13,)),
            pltpu.SemaphoreType.DMA((13,)),
        ],
        compiler_params=pltpu.CompilerParams(
            collective_id=0, has_side_effects=True, vmem_limit_bytes=56 * 1024 * 1024
        ),
    )(write_pos, lengths, query_states, key_states, value_states, queue_keys, teacher)
    return loss[0, 0], unit_vec, grad_query, grad_key, grad_value


def solution(mesh):
    placed = (
        P("grp", "ctx", None),
        P("grp", "ctx", None),
        P("grp", "ctx", None),
        P("grp"),
        P(("ctx", "grp"), None),
        P(),
        P(None, ("ctx", "grp")),
    )
    return jax.shard_map(
        shards,
        mesh=mesh,
        in_specs=placed,
        out_specs=(
            P(),
            P("grp", None),
            P("grp", "ctx", None),
            P("grp", "ctx", None),
            P("grp", "ctx", None),
        ),
        check_vma=False,
    )
```

```python
import functools

import jax
import jax.numpy as jnp
from jax import lax
from jax.experimental import pallas as pl
from jax.experimental.pallas import tpu as pltpu
from jax.sharding import PartitionSpec as P

HD = 128
HEADS = 16
GROUPS = 2
BLOCK = 128
KV = GROUPS * HD
CHIPS = 32
HALF = 8
WIDE = HALF * HD
DOCS = 8
ENTRIES = 256
NZ = 16
PLANE = 32
ROWS = 9

inverse_temp = 10.0
loss_scale = 2.0**24
norm_eps = 1e-06

MESH = pl.DeviceIdType.MESH


def position():
    ctx = lax.axis_index("ctx")
    grp = lax.axis_index("grp")
    return ctx // 32, (ctx // 2) % NZ, ctx % 2, grp


def device(x_hi, z, core, grp):
    return ((x_hi * NZ + z) * 2 + core, grp)


def shifted(dx=0, dy=0, dz=0, dc=0):
    x_hi, z, core, grp = position()
    x = (2 * x_hi + grp // 4 + dx) % 4
    return device(x // 2, (z + dz) % NZ, (core + dc) % 2, (x % 2) * 4 + (grp + dy) % 4)


def plane_peer(step):
    x_hi, z, core, grp = position()
    turn = (step // 4) % 4
    turn = turn + turn // 2 - 2 * (turn // 3)
    px = (x_hi + step // 16) % 2
    pc = (core + step % 2) % 2
    pl_x = (grp // 4 + (step // 2) % 2) % 2
    py = (grp + turn) % 4
    return px, pc, pl_x * 4 + py


def z_offset(step):
    return 8 + ((step + 1) // 2) * (2 * (step % 2) - 1)


def send_plane(src_of, dst, send_sem, recv_sem):
    x_hi, z, core, grp = position()
    mine = x_hi * 16 + core * 8 + grp

    def one(k, carry):
        px, pc, pg = plane_peer(31 - k)
        pltpu.make_async_remote_copy(
            src_ref=src_of(pc, pg),
            dst_ref=dst(mine),
            send_sem=send_sem,
            recv_sem=recv_sem,
            device_id=device(px, z, pc, pg),
            device_id_type=MESH,
        ).start()
        return carry

    lax.fori_loop(0, PLANE - 1, one, 0)


def send_ring(src, dst, send_sem, recv_sem):
    x_hi, z, core, grp = position()

    def one(k, carry):
        pltpu.make_async_remote_copy(
            src_ref=src,
            dst_ref=dst(z),
            send_sem=send_sem,
            recv_sem=recv_sem,
            device_id=device(x_hi, (z + z_offset(k)) % NZ, core, grp),
            device_id_type=MESH,
        ).start()
        return carry

    lax.fori_loop(0, NZ - 1, one, 0)


def wait_bytes(ref, sem):
    pltpu.make_async_copy(ref, ref, sem).wait()


def sum_slots(ref, count):
    total = ref[0]
    for i in range(1, count):
        total = total + ref[i]
    return total


def two_halves(x):
    high = x.astype(jnp.bfloat16).astype(jnp.float32)
    return jnp.concatenate([high, x - high], 0).astype(jnp.bfloat16)


def whole_kernel(
    pos_hbm, len_hbm, query_hbm, key_hbm, value_hbm, queue_ref, teacher_hbm,
    loss_ref, emb_ref, dq_ref, dk_ref, dv_ref,
    pos_ref, len_ref, query_out, key_out, value_out, query, keys, values, teacher_ref, prob, sums, sums_in, score,
    dk_out, dk_in, dk_chip, dk_part, dv_chip, dq_chip,
    eff, mix, zb, pb, t_out, tp, tz, t_own, t_half, s_out, ep, ez, half_sum, ring_out,
    t_ring_out, t_full, unit_rows, e_ring_out,
    ready, load_sem, send, recv, near_send, near_recv,
):
    x_hi, z, core, grp = position()
    mine = x_hi * 16 + core * 8 + grp
    ctx = (x_hi * NZ + z) * 2 + core
    chip = x_hi * NZ + z
    twin = (chip * 2 + 1 - core, grp)

    def beside(by, which):
        return ((chip + CHIPS + by) % CHIPS * 2 + which, grp)

    barrier = pltpu.get_barrier_semaphore()
    first = [shifted(dx=dx, dy=dy) for dx in (1, 3) for dy in (1, 3)]
    first += [shifted(dz=2), shifted(dz=NZ - 2), shifted(dx=2), shifted(dy=2)]
    first += [beside(by, which) for by in (1, -1) for which in (0, 1)]
    first += [shifted(dz=1), shifted(dz=NZ - 1), shifted(dx=1), shifted(dx=3), shifted(dy=1), shifted(dy=3), twin]
    for to in first:
        pl.semaphore_signal(barrier, inc=1, device_id=to, device_id_type=MESH)

    loads = []
    for i, (source, goal) in enumerate((
        (key_hbm.at[0, :, pl.ds(0, KV)], key_out.at[0]),
        (key_hbm.at[0, :, pl.ds(KV, KV)], key_out.at[1]),
        (query_hbm.at[0, :, pl.ds(0, WIDE)], query_out.at[0]),
        (query_hbm.at[0, :, pl.ds(WIDE, WIDE)], query_out.at[1]),
        (value_hbm.at[0, :, pl.ds(0, KV)], value_out.at[0]),
        (value_hbm.at[0, :, pl.ds(KV, KV)], value_out.at[1]),
        (teacher_hbm, teacher_ref),
        (queue_ref, eff),
        (key_hbm.at[0, :, pl.ds(pl.multiple_of(core * KV, KV), KV)], keys.at[2 + core]),
        (query_hbm.at[0, :, pl.ds(pl.multiple_of(core * WIDE, WIDE), WIDE)], query.at[core]),
        (value_hbm.at[0, :, pl.ds(pl.multiple_of(core * KV, KV), KV)], values.at[2 + core]),
        (pos_hbm, pos_ref),
        (len_hbm, len_ref),
    )):
        loads.append(pltpu.make_async_copy(source, goal, load_sem.at[i]))
        loads[-1].start()

    for i in range(6):
        loads[i].wait()
    pl.semaphore_wait(barrier, len(first))

    def start(source, goal, which, to):
        copy = pltpu.make_async_remote_copy(
            src_ref=source,
            dst_ref=goal,
            send_sem=near_send.at[which],
            recv_sem=near_recv.at[which],
            device_id=to,
            device_id_type=MESH,
        )
        copy.start()
        return copy

    def to_next(source, goal, which):
        for half in range(2):
            pltpu.make_async_remote_copy(
                src_ref=source.at[half],
                dst_ref=goal.at[core],
                send_sem=near_send.at[which + half],
                recv_sem=near_recv.at[which + core],
                device_id=beside(1, half),
                device_id_type=MESH,
            ).start()

    to_next(key_out, keys, 0)
    start(key_out.at[1 - core], keys.at[2 + core], 2, twin)
    start(query_out.at[1 - core], query.at[core], 3, twin)
    start(value_out.at[1 - core], values.at[2 + core], 6, twin)
    to_next(value_out, values, 4)
    for to in (shifted(dz=2), shifted(dz=NZ - 2), shifted(dx=2), shifted(dy=2), twin):
        pl.semaphore_signal(ready.at[0], inc=1, device_id=to, device_id_type=MESH)

    base = (ctx * 8 + grp) * ENTRIES
    entry = lax.broadcasted_iota(jnp.int32, (DOCS, ENTRIES), 1) + base
    lane = lax.broadcasted_iota(jnp.int32, (DOCS, 128), 1)
    row = lax.broadcasted_iota(jnp.int32, (DOCS, 128), 0)
    loads[6].wait()
    loads[11].wait()
    loads[12].wait()
    teacher = teacher_ref[...]
    kept = jnp.ones((DOCS, ENTRIES), jnp.float32)
    there = jnp.zeros((DOCS, 128), jnp.float32)
    teacher_at = jnp.zeros((DOCS, 128), jnp.float32)
    for d in range(DOCS):
        hit = (entry == pos_ref[d]).astype(jnp.float32)
        kept = kept - hit
        at = (lane == d).astype(jnp.float32)
        there = there + at * jnp.sum(hit, 1, keepdims=True)
        teacher_at = teacher_at + at * jnp.sum(teacher * hit, 1, keepdims=True)
    target = jnp.where(kept > 0, jnp.exp(teacher), 0.0)
    target_at = jnp.where(there > 0, jnp.exp(teacher_at), 0.0)
    target_sum = jnp.sum(target, 1, keepdims=True) + jnp.sum(target_at, 1, keepdims=True)
    target_row = jnp.sum(jnp.where(lane == row, target_sum, 0.0), 0, keepdims=True) + pltpu.roll(target_at, DOCS, 1)

    def spread(out, part):
        for h in range(HEADS):
            out[:, h // HALF, h % HALF] = part[:, h * HD : (h + 1) * HD]

    loads[7].wait()
    mixed = jnp.dot(two_halves(target), eff[...], preferred_element_type=jnp.float32)
    spread(t_out, mixed[:DOCS] + mixed[DOCS:])
    for c in range(2):
        t_out[:, c, HALF] = target_row

    pl.semaphore_wait(ready.at[0], 5)
    pl.semaphore_signal(ready.at[1], inc=1, device_id=twin, device_id_type=MESH)
    for to in (4, NZ - 4):
        pl.semaphore_signal(ready.at[2], inc=1, device_id=shifted(dz=to), device_id_type=MESH)

    later = lax.broadcasted_iota(jnp.int32, (BLOCK, BLOCK), 1)
    rows = lax.broadcasted_iota(jnp.int32, (BLOCK, BLOCK), 0)
    inside = (later > rows, None, later <= rows)

    def stacked(r, g):
        return jnp.concatenate([query[r, :, (4 * g + j) * HD : (4 * g + j + 1) * HD] for j in range(4)], 0)

    def weigh(r, s):
        for g in range(GROUPS):
            tile = keys[r + s, :, g * HD : (g + 1) * HD]
            scores = lax.dot_general(
                stacked(r, g), tile, (((1,), (1,)), ((), ())), preferred_element_type=jnp.float32
            )
            weight = jnp.exp(scores * HD ** (-0.5)).reshape(4, BLOCK, BLOCK)
            seen = inside[s]
            if r + s < 2:
                before = jnp.broadcast_to(chip >= 1, (BLOCK, BLOCK))
                seen = before if seen is None else seen & before
            if seen is not None:
                weight = jnp.where(seen[None], weight, 0.0)
            prob[r, 4 * g : 4 * g + 4, :, s * BLOCK : (s + 1) * BLOCK] = weight

    def arrived(ref, which):
        wait_bytes(ref, near_recv.at[which])

    for i in (8, 9, 10):
        loads[i].wait()
    arrived(key_out.at[0], 2)
    arrived(query_out.at[0], 3)
    weigh(0, 2)
    weigh(1, 1)
    weigh(1, 2)
    arrived(key_out.at[0], 0)
    arrived(key_out.at[0], 1)
    weigh(0, 0)
    weigh(0, 1)
    weigh(1, 0)

    length = len_ref[0]
    column = []
    for r in range(2):
        place = lax.broadcasted_iota(jnp.int32, (BLOCK, 1), 0) + (chip * 2 + r) * BLOCK
        live = (place < length).astype(jnp.float32)
        for h in range(HALF):
            weight = prob[r, h]
            total = weight[:, :BLOCK] + weight[:, BLOCK : 2 * BLOCK] + weight[:, 2 * BLOCK :]
            part = weight * (live / jnp.sum(total, 1, keepdims=True))
            prob[r, h] = part
            column.append(jnp.sum(part, 0, keepdims=True))
    for block in range(4):
        parts = []
        for r in range(2):
            s = block - r
            if 0 <= s < 3:
                parts.append(
                    jnp.concatenate([column[r * HALF + h][:, s * BLOCK : (s + 1) * BLOCK] for h in range(HALF)], 0)
                )
        sums[block] = parts[0] if len(parts) == 1 else parts[0] + parts[1]
    start(sums.at[pl.ds(0, 2)], sums_in, 7, beside(-1, core))

    pl.semaphore_wait(ready.at[1], 1)
    send_plane(
        lambda pc, pg: t_out.at[pg, pc, pl.ds(0, ROWS)],
        lambda me: tp.at[me, pl.ds(0, ROWS)],
        send.at[0],
        recv.at[0],
    )
    tp[mine] = t_out[grp, core]

    arrived(value_out.at[0], 6)
    arrived(sums_in, 7)
    length_float = length.astype(jnp.float32)
    sums_all = sums[pl.ds(2, 2)] + sums_in[...]
    for g in range(GROUPS):
        both = jnp.concatenate([sums_all[b, 4 * g : 4 * g + 4] for b in range(2)], 1)
        split = jnp.concatenate([both, jnp.zeros_like(both)], 0)
        tile = values[pl.ds(2, 2), :, g * HD : (g + 1) * HD].reshape(2 * BLOCK, HD)
        out = jnp.dot(two_halves(split), tile, preferred_element_type=jnp.float32)
        half_sum[4 * g : 4 * g + 4] = (out[:4] + out[8:12]) / length_float

    pl.semaphore_wait(ready.at[2], 2)
    send_ring(half_sum, lambda me: zb.at[me], send.at[2], recv.at[2])
    zb[z] = half_sum[...]

    wait_bytes(tp.at[pl.ds(0, PLANE - 1), pl.ds(0, ROWS)], recv.at[0])
    t_ring_out[...] = sum_slots(tp, PLANE)

    wait_bytes(zb.at[pl.ds(0, NZ - 1)], recv.at[2])
    ring_out[...] = sum_slots(zb, NZ)
    send_plane(lambda pc, pg: ring_out, lambda me: pb.at[me], send.at[4], recv.at[4])
    pb[mine] = ring_out[...]
    send_ring(t_ring_out.at[pl.ds(0, ROWS)], lambda me: tz.at[me, pl.ds(0, ROWS)], send.at[3], recv.at[3])
    tz[z] = t_ring_out[...]

    wait_bytes(pb.at[pl.ds(0, PLANE - 1)], recv.at[4])
    heads = []
    for c in range(2):
        both = pb[pl.ds(c * 8, 8)] + pb[pl.ds(16 + c * 8, 8)]
        unit_rows[:, pl.ds(c * HALF, HALF)] = both
    square = jnp.zeros((DOCS, HD), jnp.float32)
    for h in range(HEADS):
        tile = unit_rows[:, h]
        heads.append(tile)
        square = square + tile * tile
    root_mean = jnp.sqrt(jnp.sum(square, 1, keepdims=True) / 2048.0 + norm_eps)
    norm_scale = root_mean * 2048.0**0.5
    unit = [(heads[h] / norm_scale).astype(jnp.bfloat16) for h in range(HEADS)]
    unit16 = jnp.concatenate(unit, 1)
    unit16 = jnp.concatenate([unit16, jnp.zeros_like(unit16)], 0)
    near = (
        lax.dot_general(unit16, eff[...], (((1,), (1,)), ((), ())), preferred_element_type=jnp.float32)[:DOCS]
        * inverse_temp
    )
    unit = [x.astype(jnp.float32) for x in unit]
    far = jnp.zeros((DOCS, 128), jnp.float32)
    for d in range(DOCS):
        product = unit[0] * unit[0][d : d + 1]
        for h in range(1, HEADS):
            product = product + unit[h] * unit[h][d : d + 1]
        far = far + jnp.where(lane == d, inverse_temp * jnp.sum(product, 1, keepdims=True), 0.0)
    student = jnp.where(kept > 0, jnp.exp(near), 0.0)
    student_at = jnp.where(there > 0, jnp.exp(far), 0.0)
    student_sum = jnp.sum(student, 1, keepdims=True) + jnp.sum(student_at, 1, keepdims=True)
    cross = jnp.sum(target * (teacher - near), 1, keepdims=True) + jnp.sum(
        target_at * (teacher_at - far), 1, keepdims=True
    )
    inner = jnp.sum(student * near, 1, keepdims=True) + jnp.sum(student_at * far, 1, keepdims=True)
    extra = jnp.zeros((DOCS, 128), jnp.float32)
    for i, value in enumerate((student_sum, cross, inner)):
        extra = extra + jnp.where(lane == row + DOCS * i, value, 0.0)
    extra = jnp.broadcast_to(jnp.sum(extra, 0, keepdims=True), (DOCS, 128))
    mixed = jnp.dot(two_halves(student), eff[...], preferred_element_type=jnp.float32)
    weights = [jnp.sum(jnp.where(lane == d, student_at, 0.0), 1, keepdims=True) for d in range(DOCS)]
    for h in range(HEADS):
        tile = mixed[:DOCS, h * HD : (h + 1) * HD] + mixed[DOCS:, h * HD : (h + 1) * HD]
        for d in range(DOCS):
            tile = tile + weights[d] * unit[h][d : d + 1]
        s_out[:, h // HALF, h % HALF] = tile
    for c in range(2):
        s_out[:, c, HALF] = extra
    send_plane(
        lambda pc, pg: s_out.at[pg, pc, pl.ds(0, ROWS)], lambda me: ep.at[me, pl.ds(0, ROWS)], send.at[6], recv.at[6]
    )
    ep[mine] = s_out[grp, core]

    wait_bytes(tz.at[pl.ds(0, NZ - 1), pl.ds(0, ROWS)], recv.at[3])
    t_own[...] = sum_slots(tz, NZ)
    t_pair = pltpu.make_async_remote_copy(
        src_ref=t_own.at[pl.ds(0, HALF)],
        dst_ref=t_half,
        send_sem=send.at[5],
        recv_sem=recv.at[5],
        device_id=twin,
        device_id_type=MESH,
    )
    t_pair.start()

    own = unit_rows[grp]
    own_mean = jnp.sqrt(jnp.sum(jnp.sum(own * own, 1, keepdims=True), 0, keepdims=True) / 2048.0 + norm_eps)
    own_scale = own_mean * 2048.0**0.5
    emb = own / own_scale
    for h in range(HEADS):
        emb_ref[:, h * HD : (h + 1) * HD] = emb[h : h + 1]
    emb_half = unit_rows[grp, pl.ds(pl.multiple_of(core * HALF, HALF), HALF)] / own_scale
    t_pair.wait_recv()
    t_full[pl.ds(pl.multiple_of(core * HALF, HALF), HALF)] = t_own[pl.ds(0, HALF)]
    t_full[pl.ds(pl.multiple_of((1 - core) * HALF, HALF), HALF)] = t_half[...]
    t_sum = t_full[...]
    lane1 = lax.broadcasted_iota(jnp.int32, (1, 128), 1)
    target_row = t_own[pl.ds(HALF, 1)]
    for d in range(DOCS):
        weight = jnp.sum(jnp.where(lane1 == DOCS + d, target_row, 0.0), 1, keepdims=True)
        other = unit_rows[d]
        other_mean = jnp.sqrt(jnp.sum(jnp.sum(other * other, 1, keepdims=True), 0, keepdims=True) / 2048.0 + norm_eps)
        other_unit = (other / (other_mean * 2048.0**0.5)).astype(jnp.bfloat16).astype(jnp.float32)
        t_sum = t_sum + weight * other_unit
    target_total = jnp.sum(jnp.where(lane1 == grp, target_row, 0.0), 1, keepdims=True)
    unit_own = emb.astype(jnp.bfloat16).astype(jnp.float32)
    t_inner = jnp.sum(jnp.sum(unit_own * t_sum, 1, keepdims=True), 0, keepdims=True) / target_total
    t_full[...] = t_sum
    t_mean = t_full[pl.ds(pl.multiple_of(core * HALF, HALF), HALF)] / target_total
    mine_only = lax.broadcasted_iota(jnp.int32, (HALF, KV), 1) // HD == (
        lax.broadcasted_iota(jnp.int32, (HALF, KV), 0) // 4
    )
    arrived(value_out.at[0], 4)
    arrived(value_out.at[0], 5)

    wait_bytes(ep.at[pl.ds(0, PLANE - 1), pl.ds(0, ROWS)], recv.at[6])
    e_ring_out[...] = sum_slots(ep, PLANE)
    send_ring(e_ring_out.at[pl.ds(0, ROWS)], lambda me: ez.at[me, pl.ds(0, ROWS)], send.at[7], recv.at[7])
    ez[z] = e_ring_out[...]
    wait_bytes(ez.at[pl.ds(0, NZ - 1), pl.ds(0, ROWS)], recv.at[7])
    mix[...] = sum_slots(ez, NZ)
    student_all = mix[pl.ds(HALF, 1)]
    cross_all = pltpu.roll(student_all, 128 - DOCS, 1)
    student_total = jnp.sum(jnp.where(lane1 == grp, student_all, 0.0), 1, keepdims=True)
    s_inner = jnp.sum(jnp.where(lane1 == grp + 2 * DOCS, student_all, 0.0), 1, keepdims=True) / (
        inverse_temp * student_total
    )
    factor = inverse_temp * loss_scale / DOCS
    unit_grad = factor * (mix[pl.ds(0, HALF)] / student_total - t_mean)
    cot = (unit_grad - emb_half * (factor * (s_inner - t_inner))) / own_scale / length_float
    cot_diag = jnp.where(mine_only, jnp.concatenate([cot] * GROUPS, 1), 0.0)
    cot_diag = jnp.concatenate([cot_diag, jnp.zeros_like(cot_diag)], 0).astype(jnp.bfloat16)
    prob_grad = lax.dot_general(
        cot_diag, values[...].reshape(4 * BLOCK, KV), (((1,), (1,)), ((), ())), preferred_element_type=jnp.float32
    )

    def scored(r):
        for h in range(HALF):
            part = prob[r, h]
            push = part * prob_grad[h : h + 1, r * BLOCK : (r + 3) * BLOCK]
            total = push[:, :BLOCK] + push[:, BLOCK : 2 * BLOCK] + push[:, 2 * BLOCK :]
            score[r, h // 4, (h % 4) * BLOCK : (h % 4 + 1) * BLOCK] = (
                push - part * jnp.sum(total, 1, keepdims=True)
            ).astype(jnp.bfloat16)

    def key_grad(block, g):
        total = None
        for r in range(2):
            s = block - r
            if 0 <= s < 3:
                one = lax.dot_general(
                    score[r, g, :, s * BLOCK : (s + 1) * BLOCK],
                    stacked(r, g),
                    (((0,), (0,)), ((), ())),
                    preferred_element_type=jnp.float32,
                )
                total = one if total is None else total + one
        return total * HD ** (-0.5)

    def send_back(block):
        for g in range(GROUPS):
            dk_out[block, :, g * HD : (g + 1) * HD] = key_grad(block, g).astype(jnp.bfloat16)
        pltpu.make_async_remote_copy(
            src_ref=dk_out.at[block],
            dst_ref=dk_in.at[core],
            send_sem=near_send.at[8 + block],
            recv_sem=near_recv.at[8 + core],
            device_id=beside(-1, block),
            device_id_type=MESH,
        ).start()

    def query_grad(r):
        for g in range(GROUPS):
            tile = keys[pl.ds(r, 3), :, g * HD : (g + 1) * HD].reshape(3 * BLOCK, HD)
            dq = jnp.dot(score[r, g], tile, preferred_element_type=jnp.float32) * HD ** (-0.5)
            for j in range(4):
                h = 4 * g + j
                dq_chip[r, :, h * HD : (h + 1) * HD] = dq[j * BLOCK : (j + 1) * BLOCK].astype(jnp.bfloat16)

    scored(0)
    send_back(0)
    scored(1)
    send_back(1)
    own_wide = pl.ds(pl.multiple_of(core * WIDE, WIDE), WIDE)
    own_kv = pl.ds(pl.multiple_of(core * KV, KV), KV)
    query_grad(1 - core)
    start(dq_chip.at[1 - core], dq_ref.at[0, :, own_wide], 10, twin)
    for block in range(2):
        for g in range(GROUPS):
            dk_chip[block, :, g * HD : (g + 1) * HD] = key_grad(2 + block, g)
    start(dk_chip.at[1 - core], dk_part.at[core], 11, twin)
    for block in range(2):
        high = sums_all[block].astype(jnp.bfloat16).astype(jnp.float32)
        dv_chip[block] = lax.dot_general(
            jnp.concatenate([high, sums_all[block] - high], 0).astype(jnp.bfloat16),
            jnp.concatenate([cot_diag[:HALF], cot_diag[:HALF]], 0),
            (((0,), (0,)), ((), ())),
            preferred_element_type=jnp.float32,
        ).astype(jnp.bfloat16)
    start(dv_chip.at[1 - core], dv_ref.at[0, :, own_kv], 12, twin)
    query_grad(core)
    stays = [
        pltpu.make_async_copy(dq_chip.at[core], dq_ref.at[0, :, own_wide], load_sem.at[0]),
        pltpu.make_async_copy(dv_chip.at[core], dv_ref.at[0, :, own_kv], load_sem.at[1]),
    ]
    for copy in stays:
        copy.start()
    dk_part[core] = dk_chip[core]
    terms = jnp.where(
        lane1 < DOCS,
        cross_all / jnp.where(lane1 < DOCS, target_row, 1.0)
        - jnp.log(jnp.where(lane1 < DOCS, target_row, 1.0))
        + jnp.log(jnp.where(lane1 < DOCS, student_all, 1.0)),
        0.0,
    )
    loss_ref[...] = jnp.broadcast_to(jnp.sum(terms, 1, keepdims=True) / DOCS, (1, 128))
    arrived(dk_chip.at[0], 11)
    for half in range(2):
        arrived(dk_out.at[0], 8 + half)
        dk_ref[0, :, half * KV : (half + 1) * KV] = (dk_part[half] + dk_in[half].astype(jnp.float32)).astype(
            jnp.bfloat16
        )

    arrived(dq_chip.at[0], 10)
    arrived(dv_chip.at[0], 12)
    for copy in stays:
        copy.wait()
    for ref, which in (
        (key_out.at[0], 0), (key_out.at[0], 1), (key_out.at[0], 2), (query_out.at[0], 3), (value_out.at[0], 4),
        (value_out.at[0], 5), (value_out.at[0], 6), (sums_in, 7), (dk_out.at[0], 8), (dk_out.at[0], 9),
        (dq_chip.at[0], 10), (dk_chip.at[0], 11), (dv_chip.at[0], 12),
    ):
        wait_bytes(ref, near_send.at[which])
    wait_bytes(tp.at[pl.ds(0, PLANE - 1), pl.ds(0, ROWS)], send.at[0])
    wait_bytes(zb.at[pl.ds(0, NZ - 1)], send.at[2])
    wait_bytes(tz.at[pl.ds(0, NZ - 1), pl.ds(0, ROWS)], send.at[3])
    wait_bytes(pb.at[pl.ds(0, PLANE - 1)], send.at[4])
    t_pair.wait_send()
    wait_bytes(ep.at[pl.ds(0, PLANE - 1), pl.ds(0, ROWS)], send.at[6])
    wait_bytes(ez.at[pl.ds(0, NZ - 1), pl.ds(0, ROWS)], send.at[7])


def finish_kernel(loss_in, emb_in, dq_in, dk_in, dv_in, loss_out, emb_out, dq_out, dk_out, dv_out, sem):
    pairs = ((dq_in, dq_out), (dk_in, dk_out), (dv_in, dv_out), (emb_in, emb_out))
    copies = [pltpu.make_async_copy(source, goal, sem.at[i]) for i, (source, goal) in enumerate(pairs)]
    for copy in copies:
        copy.start()
    loss_out[...] = loss_in[:, :1]
    for copy in copies:
        copy.wait()


def finish(loss, *arrays):
    vmem = pl.BlockSpec(memory_space=pltpu.VMEM)
    shapes = [jax.ShapeDtypeStruct((1, 1), jnp.float32)] + [jax.ShapeDtypeStruct(x.shape, x.dtype) for x in arrays]
    return pl.pallas_call(
        finish_kernel,
        name="finish",
        out_shape=tuple(shapes),
        in_specs=[vmem] * 5,
        out_specs=(vmem,) + (pl.BlockSpec(memory_space=pl.ANY),) * 4,
        scratch_shapes=[pltpu.SemaphoreType.DMA((4,))],
        compiler_params=pltpu.CompilerParams(vmem_limit_bytes=4 * 1024 * 1024),
    )(loss, *arrays)


def shards(query_states, key_states, value_states, lengths, queue_keys, write_pos, teacher):
    vmem = pl.BlockSpec(memory_space=pltpu.VMEM)
    in_hbm = pl.BlockSpec(memory_space=pltpu.HBM)
    anywhere = pl.BlockSpec(memory_space=pl.ANY)

    def f32(*shape):
        return pltpu.VMEM(shape, jnp.float32)

    def b16(*shape):
        return pltpu.VMEM(shape, jnp.bfloat16)

    held = [
        pltpu.with_memory_space_constraint(x, pltpu.HBM)
        for x in (write_pos, query_states, key_states, value_states, queue_keys, teacher)
    ]
    results = pl.pallas_call(
        whole_kernel,
        name="whole",
        out_shape=(
            pltpu.VMEM((1, 128), jnp.float32),
            pltpu.VMEM((1, HEADS * HD), jnp.float32),
            pltpu.VMEM(query_states.shape, jnp.bfloat16),
            pltpu.VMEM(key_states.shape, jnp.bfloat16),
            pltpu.VMEM(value_states.shape, jnp.bfloat16),
        ),
        in_specs=[in_hbm, anywhere] + [in_hbm] * 5,
        out_specs=(vmem, vmem, anywhere, vmem, anywhere),
        scratch_shapes=[
            pltpu.SMEM((DOCS,), jnp.int32),
            pltpu.SMEM((1,), jnp.int32),
            b16(2, BLOCK, WIDE),
            b16(2, BLOCK, KV),
            b16(2, BLOCK, KV),
            b16(2, BLOCK, WIDE),
            b16(4, BLOCK, KV),
            b16(4, BLOCK, KV),
            f32(DOCS, ENTRIES),
            f32(2, HALF, BLOCK, 3 * BLOCK),
            f32(4, HALF, BLOCK),
            f32(2, HALF, BLOCK),
            b16(2, GROUPS, 4 * BLOCK, 3 * BLOCK),
            b16(2, BLOCK, KV),
            b16(2, BLOCK, KV),
            f32(2, BLOCK, KV),
            f32(2, BLOCK, KV),
            b16(2, BLOCK, KV),
            b16(2, BLOCK, WIDE),
            b16(ENTRIES, 2048),
            f32(16, 128),
            f32(NZ, HALF, 128),
            f32(PLANE, HALF, 128),
            f32(DOCS, 2, 16, 128),
            f32(PLANE, 16, 128),
            f32(NZ, 16, 128),
            f32(16, 128),
            f32(HALF, 128),
            f32(DOCS, 2, 16, 128),
            f32(PLANE, 16, 128),
            f32(NZ, 16, 128),
            f32(HALF, 128),
            f32(HALF, 128),
            f32(16, 128),
            f32(HEADS, 128),
            f32(DOCS, HEADS, 128),
            f32(16, 128),
            pltpu.SemaphoreType.REGULAR((3,)),
            pltpu.SemaphoreType.DMA((13,)),
            pltpu.SemaphoreType.DMA((8,)),
            pltpu.SemaphoreType.DMA((8,)),
            pltpu.SemaphoreType.DMA((13,)),
            pltpu.SemaphoreType.DMA((13,)),
        ],
        compiler_params=pltpu.CompilerParams(
            collective_id=0, has_side_effects=True, vmem_limit_bytes=40 * 1024 * 1024
        ),
    )(held[0], lengths, *held[1:])
    loss, unit_vec, grad_query, grad_key, grad_value = finish(*results)
    return loss[0, 0], unit_vec, grad_query, grad_key, grad_value


def solution(mesh):
    placed = (
        P("grp", "ctx", None),
        P("grp", "ctx", None),
        P("grp", "ctx", None),
        P("grp"),
        P(("ctx", "grp"), None),
        P(),
        P(None, ("ctx", "grp")),
    )
    return jax.shard_map(
        shards,
        mesh=mesh,
        in_specs=placed,
        out_specs=(
            P(),
            P("grp", None),
            P("grp", "ctx", None),
            P("grp", "ctx", None),
            P("grp", "ctx", None),
        ),
        check_vma=False,
    )
```

```python
import functools

import jax
import jax.numpy as jnp
from jax import lax
from jax.experimental import pallas as pl
from jax.experimental.pallas import tpu as pltpu
from jax.sharding import PartitionSpec as P

HD = 128
HEADS = 16
GROUPS = 2
BLOCK = 128
KV = GROUPS * HD
CHIPS = 32
HALF = 8
WIDE = HALF * HD
DOCS = 8
ENTRIES = 256
NZ = 16
PLANE = 32
ROWS = 9

inverse_temp = 10.0
loss_scale = 2.0**24
norm_eps = 1e-06

MESH = pl.DeviceIdType.MESH


def position():
    ctx = lax.axis_index("ctx")
    grp = lax.axis_index("grp")
    return ctx // 32, (ctx // 2) % NZ, ctx % 2, grp


def device(x_hi, z, core, grp):
    return ((x_hi * NZ + z) * 2 + core, grp)


def shifted(dx=0, dy=0, dz=0, dc=0):
    x_hi, z, core, grp = position()
    x = (2 * x_hi + grp // 4 + dx) % 4
    return device(x // 2, (z + dz) % NZ, (core + dc) % 2, (x % 2) * 4 + (grp + dy) % 4)


def plane_peer(step):
    x_hi, z, core, grp = position()
    turn = (step // 4) % 4
    turn = turn + turn // 2 - 2 * (turn // 3)
    px = (x_hi + step // 16) % 2
    pc = (core + step % 2) % 2
    pl_x = (grp // 4 + (step // 2) % 2) % 2
    py = (grp + turn) % 4
    return px, pc, pl_x * 4 + py


def z_offset(step):
    return 8 + ((step + 1) // 2) * (2 * (step % 2) - 1)


def send_plane(src_of, dst, send_sem, recv_sem):
    x_hi, z, core, grp = position()
    mine = x_hi * 16 + core * 8 + grp

    def one(k, carry):
        px, pc, pg = plane_peer(31 - k)
        pltpu.make_async_remote_copy(
            src_ref=src_of(pc, pg),
            dst_ref=dst(mine),
            send_sem=send_sem,
            recv_sem=recv_sem,
            device_id=device(px, z, pc, pg),
            device_id_type=MESH,
        ).start()
        return carry

    lax.fori_loop(0, PLANE - 1, one, 0)


def send_ring(src, dst, send_sem, recv_sem):
    x_hi, z, core, grp = position()

    def one(k, carry):
        pltpu.make_async_remote_copy(
            src_ref=src,
            dst_ref=dst(z),
            send_sem=send_sem,
            recv_sem=recv_sem,
            device_id=device(x_hi, (z + z_offset(k)) % NZ, core, grp),
            device_id_type=MESH,
        ).start()
        return carry

    lax.fori_loop(0, NZ - 1, one, 0)


def wait_bytes(ref, sem):
    pltpu.make_async_copy(ref, ref, sem).wait()


def sum_slots(ref, count):
    total = ref[0]
    for i in range(1, count):
        total = total + ref[i]
    return total


def two_halves(x):
    high = x.astype(jnp.bfloat16).astype(jnp.float32)
    return jnp.concatenate([high, x - high], 0).astype(jnp.bfloat16)


def whole_kernel(
    pos_hbm, len_hbm, query_hbm, key_hbm, value_hbm, queue_ref, teacher_hbm,
    loss_ref, emb_ref, dq_ref, dk_ref, dv_ref,
    pos_ref, len_ref, query, keys, values, teacher_ref, prob, sums, sums_in, score,
    dk_out, dk_in, dk_chip, dk_part, dv_chip, dq_chip,
    eff, mix, zb, pb, t_out, tp, tz, t_own, t_half, s_out, ep, ez, half_sum, ring_out,
    t_ring_out, t_full, unit_rows, e_ring_out,
    ready, load_sem, send, recv, near_send, near_recv,
):
    x_hi, z, core, grp = position()
    mine = x_hi * 16 + core * 8 + grp
    ctx = (x_hi * NZ + z) * 2 + core
    chip = x_hi * NZ + z
    twin = (chip * 2 + 1 - core, grp)

    def beside(by, which):
        return ((chip + CHIPS + by) % CHIPS * 2 + which, grp)

    barrier = pltpu.get_barrier_semaphore()
    first = [shifted(dx=dx, dy=dy) for dx in (1, 3) for dy in (1, 3)]
    first += [shifted(dz=2), shifted(dz=NZ - 2), shifted(dx=2), shifted(dy=2)]
    first += [beside(by, which) for by in (1, -1) for which in (0, 1)]
    first += [shifted(dz=1), shifted(dz=NZ - 1), shifted(dx=1), shifted(dx=3), shifted(dy=1), shifted(dy=3), twin]
    for to in first:
        pl.semaphore_signal(barrier, inc=1, device_id=to, device_id_type=MESH)

    loads = []
    for i, (source, goal) in enumerate((
        (teacher_hbm, teacher_ref),
        (queue_ref, eff),
        (key_hbm.at[0, :, pl.ds(pl.multiple_of(core * KV, KV), KV)], keys.at[2 + core]),
        (query_hbm.at[0, :, pl.ds(pl.multiple_of(core * WIDE, WIDE), WIDE)], query.at[core]),
        (value_hbm.at[0, :, pl.ds(pl.multiple_of(core * KV, KV), KV)], values.at[2 + core]),
        (pos_hbm, pos_ref),
        (len_hbm, len_ref),
    )):
        loads.append(pltpu.make_async_copy(source, goal, load_sem.at[i]))
        loads[-1].start()

    pl.semaphore_wait(barrier, len(first))

    def start(source, goal, which, to):
        copy = pltpu.make_async_remote_copy(
            src_ref=source,
            dst_ref=goal,
            send_sem=near_send.at[which],
            recv_sem=near_recv.at[which],
            device_id=to,
            device_id_type=MESH,
        )
        copy.start()
        return copy

    def to_next(source, goal, which):
        for half in range(2):
            pltpu.make_async_remote_copy(
                src_ref=source.at[0, :, pl.ds(half * KV, KV)],
                dst_ref=goal.at[core],
                send_sem=near_send.at[which + half],
                recv_sem=near_recv.at[which + core],
                device_id=beside(1, half),
                device_id_type=MESH,
            ).start()

    other_kv = pl.ds(pl.multiple_of((1 - core) * KV, KV), KV)
    other_wide = pl.ds(pl.multiple_of((1 - core) * WIDE, WIDE), WIDE)
    to_next(key_hbm, keys, 0)
    start(key_hbm.at[0, :, other_kv], keys.at[2 + core], 2, twin)
    start(query_hbm.at[0, :, other_wide], query.at[core], 3, twin)
    start(value_hbm.at[0, :, other_kv], values.at[2 + core], 6, twin)
    to_next(value_hbm, values, 4)
    for to in (shifted(dz=2), shifted(dz=NZ - 2), shifted(dx=2), shifted(dy=2), twin):
        pl.semaphore_signal(ready.at[0], inc=1, device_id=to, device_id_type=MESH)

    base = (ctx * 8 + grp) * ENTRIES
    entry = lax.broadcasted_iota(jnp.int32, (DOCS, ENTRIES), 1) + base
    lane = lax.broadcasted_iota(jnp.int32, (DOCS, 128), 1)
    row = lax.broadcasted_iota(jnp.int32, (DOCS, 128), 0)
    loads[0].wait()
    loads[5].wait()
    loads[6].wait()
    teacher = teacher_ref[...]
    kept = jnp.ones((DOCS, ENTRIES), jnp.float32)
    there = jnp.zeros((DOCS, 128), jnp.float32)
    teacher_at = jnp.zeros((DOCS, 128), jnp.float32)
    for d in range(DOCS):
        hit = (entry == pos_ref[d]).astype(jnp.float32)
        kept = kept - hit
        at = (lane == d).astype(jnp.float32)
        there = there + at * jnp.sum(hit, 1, keepdims=True)
        teacher_at = teacher_at + at * jnp.sum(teacher * hit, 1, keepdims=True)
    target = jnp.where(kept > 0, jnp.exp(teacher), 0.0)
    target_at = jnp.where(there > 0, jnp.exp(teacher_at), 0.0)
    target_sum = jnp.sum(target, 1, keepdims=True) + jnp.sum(target_at, 1, keepdims=True)
    target_row = jnp.sum(jnp.where(lane == row, target_sum, 0.0), 0, keepdims=True) + pltpu.roll(target_at, DOCS, 1)

    def spread(out, part):
        for h in range(HEADS):
            out[:, h // HALF, h % HALF] = part[:, h * HD : (h + 1) * HD]

    loads[1].wait()
    mixed = jnp.dot(two_halves(target), eff[...], preferred_element_type=jnp.float32)
    spread(t_out, mixed[:DOCS] + mixed[DOCS:])
    for c in range(2):
        t_out[:, c, HALF] = target_row

    pl.semaphore_wait(ready.at[0], 5)
    pl.semaphore_signal(ready.at[1], inc=1, device_id=twin, device_id_type=MESH)
    for to in (4, NZ - 4):
        pl.semaphore_signal(ready.at[2], inc=1, device_id=shifted(dz=to), device_id_type=MESH)

    later = lax.broadcasted_iota(jnp.int32, (BLOCK, BLOCK), 1)
    rows = lax.broadcasted_iota(jnp.int32, (BLOCK, BLOCK), 0)
    inside = (later > rows, None, later <= rows)

    def stacked(r, g):
        return jnp.concatenate([query[r, :, (4 * g + j) * HD : (4 * g + j + 1) * HD] for j in range(4)], 0)

    def weigh(r, s):
        for g in range(GROUPS):
            tile = keys[r + s, :, g * HD : (g + 1) * HD]
            scores = lax.dot_general(
                stacked(r, g), tile, (((1,), (1,)), ((), ())), preferred_element_type=jnp.float32
            )
            weight = jnp.exp(scores * HD ** (-0.5)).reshape(4, BLOCK, BLOCK)
            seen = inside[s]
            if r + s < 2:
                before = jnp.broadcast_to(chip >= 1, (BLOCK, BLOCK))
                seen = before if seen is None else seen & before
            if seen is not None:
                weight = jnp.where(seen[None], weight, 0.0)
            prob[r, 4 * g : 4 * g + 4, :, s * BLOCK : (s + 1) * BLOCK] = weight

    def arrived(ref, which):
        wait_bytes(ref, near_recv.at[which])

    for i in (2, 3, 4):
        loads[i].wait()
    arrived(keys.at[0], 2)
    arrived(query.at[0], 3)
    weigh(0, 2)
    weigh(1, 1)
    weigh(1, 2)
    arrived(keys.at[0], 0)
    arrived(keys.at[0], 1)
    weigh(0, 0)
    weigh(0, 1)
    weigh(1, 0)

    length = len_ref[0]
    column = []
    for r in range(2):
        place = lax.broadcasted_iota(jnp.int32, (BLOCK, 1), 0) + (chip * 2 + r) * BLOCK
        live = (place < length).astype(jnp.float32)
        for h in range(HALF):
            weight = prob[r, h]
            total = weight[:, :BLOCK] + weight[:, BLOCK : 2 * BLOCK] + weight[:, 2 * BLOCK :]
            part = weight * (live / jnp.sum(total, 1, keepdims=True))
            prob[r, h] = part
            column.append(jnp.sum(part, 0, keepdims=True))
    for block in range(4):
        parts = []
        for r in range(2):
            s = block - r
            if 0 <= s < 3:
                parts.append(
                    jnp.concatenate([column[r * HALF + h][:, s * BLOCK : (s + 1) * BLOCK] for h in range(HALF)], 0)
                )
        sums[block] = parts[0] if len(parts) == 1 else parts[0] + parts[1]
    start(sums.at[pl.ds(0, 2)], sums_in, 7, beside(-1, core))

    pl.semaphore_wait(ready.at[1], 1)
    send_plane(
        lambda pc, pg: t_out.at[pg, pc, pl.ds(0, ROWS)],
        lambda me: tp.at[me, pl.ds(0, ROWS)],
        send.at[0],
        recv.at[0],
    )
    tp[mine] = t_out[grp, core]

    length_float = length.astype(jnp.float32)
    for which in (6, 4, 5):
        arrived(values.at[0], which)
    for g in range(GROUPS):
        both = jnp.concatenate([sums[b, 4 * g : 4 * g + 4] for b in range(4)], 1)
        split = jnp.concatenate([both, jnp.zeros_like(both)], 0)
        tile = values[:, :, g * HD : (g + 1) * HD].reshape(4 * BLOCK, HD)
        out = jnp.dot(two_halves(split), tile, preferred_element_type=jnp.float32)
        half_sum[4 * g : 4 * g + 4] = (out[:4] + out[8:12]) / length_float

    pl.semaphore_wait(ready.at[2], 2)
    send_ring(half_sum, lambda me: zb.at[me], send.at[2], recv.at[2])
    zb[z] = half_sum[...]

    wait_bytes(tp.at[pl.ds(0, PLANE - 1), pl.ds(0, ROWS)], recv.at[0])
    t_ring_out[...] = sum_slots(tp, PLANE)

    wait_bytes(zb.at[pl.ds(0, NZ - 1)], recv.at[2])
    ring_out[...] = sum_slots(zb, NZ)
    send_plane(lambda pc, pg: ring_out, lambda me: pb.at[me], send.at[4], recv.at[4])
    pb[mine] = ring_out[...]
    send_ring(t_ring_out.at[pl.ds(0, ROWS)], lambda me: tz.at[me, pl.ds(0, ROWS)], send.at[3], recv.at[3])
    tz[z] = t_ring_out[...]

    wait_bytes(pb.at[pl.ds(0, PLANE - 1)], recv.at[4])
    heads = []
    for c in range(2):
        both = pb[pl.ds(c * 8, 8)] + pb[pl.ds(16 + c * 8, 8)]
        unit_rows[:, pl.ds(c * HALF, HALF)] = both
    square = jnp.zeros((DOCS, HD), jnp.float32)
    for h in range(HEADS):
        tile = unit_rows[:, h]
        heads.append(tile)
        square = square + tile * tile
    root_mean = jnp.sqrt(jnp.sum(square, 1, keepdims=True) / 2048.0 + norm_eps)
    norm_scale = root_mean * 2048.0**0.5
    unit = [(heads[h] / norm_scale).astype(jnp.bfloat16) for h in range(HEADS)]
    unit16 = jnp.concatenate(unit, 1)
    unit16 = jnp.concatenate([unit16, jnp.zeros_like(unit16)], 0)
    near = (
        lax.dot_general(unit16, eff[...], (((1,), (1,)), ((), ())), preferred_element_type=jnp.float32)[:DOCS]
        * inverse_temp
    )
    unit = [x.astype(jnp.float32) for x in unit]
    far = jnp.zeros((DOCS, 128), jnp.float32)
    for d in range(DOCS):
        product = unit[0] * unit[0][d : d + 1]
        for h in range(1, HEADS):
            product = product + unit[h] * unit[h][d : d + 1]
        far = far + jnp.where(lane == d, inverse_temp * jnp.sum(product, 1, keepdims=True), 0.0)
    student = jnp.where(kept > 0, jnp.exp(near), 0.0)
    student_at = jnp.where(there > 0, jnp.exp(far), 0.0)
    student_sum = jnp.sum(student, 1, keepdims=True) + jnp.sum(student_at, 1, keepdims=True)
    cross = jnp.sum(target * (teacher - near), 1, keepdims=True) + jnp.sum(
        target_at * (teacher_at - far), 1, keepdims=True
    )
    inner = jnp.sum(student * near, 1, keepdims=True) + jnp.sum(student_at * far, 1, keepdims=True)
    extra = jnp.zeros((DOCS, 128), jnp.float32)
    for i, value in enumerate((student_sum, cross, inner)):
        extra = extra + jnp.where(lane == row + DOCS * i, value, 0.0)
    extra = jnp.broadcast_to(jnp.sum(extra, 0, keepdims=True), (DOCS, 128))
    mixed = jnp.dot(two_halves(student), eff[...], preferred_element_type=jnp.float32)
    weights = [jnp.sum(jnp.where(lane == d, student_at, 0.0), 1, keepdims=True) for d in range(DOCS)]
    for h in range(HEADS):
        tile = mixed[:DOCS, h * HD : (h + 1) * HD] + mixed[DOCS:, h * HD : (h + 1) * HD]
        for d in range(DOCS):
            tile = tile + weights[d] * unit[h][d : d + 1]
        s_out[:, h // HALF, h % HALF] = tile
    for c in range(2):
        s_out[:, c, HALF] = extra
    send_plane(
        lambda pc, pg: s_out.at[pg, pc, pl.ds(0, ROWS)], lambda me: ep.at[me, pl.ds(0, ROWS)], send.at[6], recv.at[6]
    )
    ep[mine] = s_out[grp, core]

    wait_bytes(tz.at[pl.ds(0, NZ - 1), pl.ds(0, ROWS)], recv.at[3])
    t_own[...] = sum_slots(tz, NZ)
    t_pair = pltpu.make_async_remote_copy(
        src_ref=t_own.at[pl.ds(0, HALF)],
        dst_ref=t_half,
        send_sem=send.at[5],
        recv_sem=recv.at[5],
        device_id=twin,
        device_id_type=MESH,
    )
    t_pair.start()

    own = unit_rows[grp]
    own_mean = jnp.sqrt(jnp.sum(jnp.sum(own * own, 1, keepdims=True), 0, keepdims=True) / 2048.0 + norm_eps)
    own_scale = own_mean * 2048.0**0.5
    emb = own / own_scale
    for h in range(HEADS):
        emb_ref[:, h * HD : (h + 1) * HD] = emb[h : h + 1]
    emb_half = unit_rows[grp, pl.ds(pl.multiple_of(core * HALF, HALF), HALF)] / own_scale
    t_pair.wait_recv()
    t_full[pl.ds(pl.multiple_of(core * HALF, HALF), HALF)] = t_own[pl.ds(0, HALF)]
    t_full[pl.ds(pl.multiple_of((1 - core) * HALF, HALF), HALF)] = t_half[...]
    t_sum = t_full[...]
    lane1 = lax.broadcasted_iota(jnp.int32, (1, 128), 1)
    target_row = t_own[pl.ds(HALF, 1)]
    for d in range(DOCS):
        weight = jnp.sum(jnp.where(lane1 == DOCS + d, target_row, 0.0), 1, keepdims=True)
        other = unit_rows[d]
        other_mean = jnp.sqrt(jnp.sum(jnp.sum(other * other, 1, keepdims=True), 0, keepdims=True) / 2048.0 + norm_eps)
        other_unit = (other / (other_mean * 2048.0**0.5)).astype(jnp.bfloat16).astype(jnp.float32)
        t_sum = t_sum + weight * other_unit
    target_total = jnp.sum(jnp.where(lane1 == grp, target_row, 0.0), 1, keepdims=True)
    unit_own = emb.astype(jnp.bfloat16).astype(jnp.float32)
    t_inner = jnp.sum(jnp.sum(unit_own * t_sum, 1, keepdims=True), 0, keepdims=True) / target_total
    t_full[...] = t_sum
    t_mean = t_full[pl.ds(pl.multiple_of(core * HALF, HALF), HALF)] / target_total
    mine_only = lax.broadcasted_iota(jnp.int32, (HALF, KV), 1) // HD == (
        lax.broadcasted_iota(jnp.int32, (HALF, KV), 0) // 4
    )
    arrived(sums_in, 7)
    sums_all = sums[pl.ds(2, 2)] + sums_in[...]

    wait_bytes(ep.at[pl.ds(0, PLANE - 1), pl.ds(0, ROWS)], recv.at[6])
    e_ring_out[...] = sum_slots(ep, PLANE)
    send_ring(e_ring_out.at[pl.ds(0, ROWS)], lambda me: ez.at[me, pl.ds(0, ROWS)], send.at[7], recv.at[7])
    ez[z] = e_ring_out[...]
    wait_bytes(ez.at[pl.ds(0, NZ - 1), pl.ds(0, ROWS)], recv.at[7])
    mix[...] = sum_slots(ez, NZ)
    student_all = mix[pl.ds(HALF, 1)]
    cross_all = pltpu.roll(student_all, 128 - DOCS, 1)
    student_total = jnp.sum(jnp.where(lane1 == grp, student_all, 0.0), 1, keepdims=True)
    s_inner = jnp.sum(jnp.where(lane1 == grp + 2 * DOCS, student_all, 0.0), 1, keepdims=True) / (
        inverse_temp * student_total
    )
    factor = inverse_temp * loss_scale / DOCS
    unit_grad = factor * (mix[pl.ds(0, HALF)] / student_total - t_mean)
    cot = (unit_grad - emb_half * (factor * (s_inner - t_inner))) / own_scale / length_float
    cot_diag = jnp.where(mine_only, jnp.concatenate([cot] * GROUPS, 1), 0.0)
    cot_diag = jnp.concatenate([cot_diag, jnp.zeros_like(cot_diag)], 0).astype(jnp.bfloat16)
    prob_grad = lax.dot_general(
        cot_diag, values[...].reshape(4 * BLOCK, KV), (((1,), (1,)), ((), ())), preferred_element_type=jnp.float32
    )

    def scored(r, g):
        for h in range(4 * g, 4 * g + 4):
            part = prob[r, h]
            push = part * prob_grad[h : h + 1, r * BLOCK : (r + 3) * BLOCK]
            total = push[:, :BLOCK] + push[:, BLOCK : 2 * BLOCK] + push[:, 2 * BLOCK :]
            score[r, g, (h % 4) * BLOCK : (h % 4 + 1) * BLOCK] = (
                push - part * jnp.sum(total, 1, keepdims=True)
            ).astype(jnp.bfloat16)

    def key_grad(block, g):
        total = None
        for r in range(2):
            s = block - r
            if 0 <= s < 3:
                one = lax.dot_general(
                    score[r, g, :, s * BLOCK : (s + 1) * BLOCK],
                    stacked(r, g),
                    (((0,), (0,)), ((), ())),
                    preferred_element_type=jnp.float32,
                )
                total = one if total is None else total + one
        return total * HD ** (-0.5)

    def send_back(block, g):
        dk_out[block, g] = key_grad(block, g).astype(jnp.bfloat16)
        pltpu.make_async_remote_copy(
            src_ref=dk_out.at[block, g],
            dst_ref=dk_in.at[core, g],
            send_sem=near_send.at[8 + block],
            recv_sem=near_recv.at[8 + core],
            device_id=beside(-1, block),
            device_id_type=MESH,
        ).start()

    def query_grad(r):
        for g in range(GROUPS):
            tile = keys[pl.ds(r, 3), :, g * HD : (g + 1) * HD].reshape(3 * BLOCK, HD)
            dq = jnp.dot(score[r, g], tile, preferred_element_type=jnp.float32) * HD ** (-0.5)
            for j in range(4):
                h = 4 * g + j
                dq_chip[r, :, h * HD : (h + 1) * HD] = dq[j * BLOCK : (j + 1) * BLOCK].astype(jnp.bfloat16)

    for r in range(2):
        for g in range(GROUPS):
            scored(r, g)
            send_back(r, g)
    own_wide = pl.ds(pl.multiple_of(core * WIDE, WIDE), WIDE)
    own_kv = pl.ds(pl.multiple_of(core * KV, KV), KV)
    query_grad(1 - core)
    start(dq_chip.at[1 - core], dq_ref.at[0, :, own_wide], 10, twin)
    for block in range(2):
        for g in range(GROUPS):
            dk_chip[block, :, g * HD : (g + 1) * HD] = key_grad(2 + block, g)
    start(dk_chip.at[1 - core], dk_part.at[core], 11, twin)
    for block in range(2):
        high = sums_all[block].astype(jnp.bfloat16).astype(jnp.float32)
        dv_chip[block] = lax.dot_general(
            jnp.concatenate([high, sums_all[block] - high], 0).astype(jnp.bfloat16),
            jnp.concatenate([cot_diag[:HALF], cot_diag[:HALF]], 0),
            (((0,), (0,)), ((), ())),
            preferred_element_type=jnp.float32,
        ).astype(jnp.bfloat16)
    start(dv_chip.at[1 - core], dv_ref.at[0, :, own_kv], 12, twin)
    query_grad(core)
    stays = [
        pltpu.make_async_copy(dq_chip.at[core], dq_ref.at[0, :, own_wide], load_sem.at[0]),
        pltpu.make_async_copy(dv_chip.at[core], dv_ref.at[0, :, own_kv], load_sem.at[1]),
    ]
    for copy in stays:
        copy.start()
    dk_part[core] = dk_chip[core]
    terms = jnp.where(
        lane1 < DOCS,
        cross_all / jnp.where(lane1 < DOCS, target_row, 1.0)
        - jnp.log(jnp.where(lane1 < DOCS, target_row, 1.0))
        + jnp.log(jnp.where(lane1 < DOCS, student_all, 1.0)),
        0.0,
    )
    loss_ref[...] = jnp.broadcast_to(jnp.sum(terms, 1, keepdims=True) / DOCS, (1, 128))
    arrived(dk_chip.at[0], 11)
    for half in range(2):
        arrived(dk_out.at[0], 8 + half)
        arrived_part = jnp.concatenate([dk_in[half, g] for g in range(GROUPS)], 1).astype(jnp.float32)
        dk_ref[0, :, half * KV : (half + 1) * KV] = (dk_part[half] + arrived_part).astype(jnp.bfloat16)

    arrived(dq_chip.at[0], 10)
    arrived(dv_chip.at[0], 12)
    for copy in stays:
        copy.wait()
    for ref, which in (
        (keys.at[0], 0), (keys.at[0], 1), (keys.at[0], 2), (query.at[0], 3), (values.at[0], 4),
        (values.at[0], 5), (values.at[0], 6), (sums_in, 7), (dk_out.at[0], 8), (dk_out.at[0], 9),
        (dq_chip.at[0], 10), (dk_chip.at[0], 11), (dv_chip.at[0], 12),
    ):
        wait_bytes(ref, near_send.at[which])
    wait_bytes(tp.at[pl.ds(0, PLANE - 1), pl.ds(0, ROWS)], send.at[0])
    wait_bytes(zb.at[pl.ds(0, NZ - 1)], send.at[2])
    wait_bytes(tz.at[pl.ds(0, NZ - 1), pl.ds(0, ROWS)], send.at[3])
    wait_bytes(pb.at[pl.ds(0, PLANE - 1)], send.at[4])
    t_pair.wait_send()
    wait_bytes(ep.at[pl.ds(0, PLANE - 1), pl.ds(0, ROWS)], send.at[6])
    wait_bytes(ez.at[pl.ds(0, NZ - 1), pl.ds(0, ROWS)], send.at[7])


def finish_kernel(loss_in, emb_in, dq_in, dk_in, dv_in, loss_out, emb_out, dq_out, dk_out, dv_out, sem):
    pairs = ((dq_in, dq_out), (dk_in, dk_out), (dv_in, dv_out), (emb_in, emb_out))
    copies = [pltpu.make_async_copy(source, goal, sem.at[i]) for i, (source, goal) in enumerate(pairs)]
    for copy in copies:
        copy.start()
    loss_out[...] = loss_in[:, :1]
    for copy in copies:
        copy.wait()


def finish(loss, *arrays):
    vmem = pl.BlockSpec(memory_space=pltpu.VMEM)
    shapes = [jax.ShapeDtypeStruct((1, 1), jnp.float32)] + [jax.ShapeDtypeStruct(x.shape, x.dtype) for x in arrays]
    return pl.pallas_call(
        finish_kernel,
        name="finish",
        out_shape=tuple(shapes),
        in_specs=[vmem] * 5,
        out_specs=(vmem,) + (pl.BlockSpec(memory_space=pl.ANY),) * 4,
        scratch_shapes=[pltpu.SemaphoreType.DMA((4,))],
        compiler_params=pltpu.CompilerParams(vmem_limit_bytes=4 * 1024 * 1024),
    )(loss, *arrays)


def shards(query_states, key_states, value_states, lengths, queue_keys, write_pos, teacher):
    vmem = pl.BlockSpec(memory_space=pltpu.VMEM)
    in_hbm = pl.BlockSpec(memory_space=pltpu.HBM)
    anywhere = pl.BlockSpec(memory_space=pl.ANY)

    def f32(*shape):
        return pltpu.VMEM(shape, jnp.float32)

    def b16(*shape):
        return pltpu.VMEM(shape, jnp.bfloat16)

    held = [
        pltpu.with_memory_space_constraint(x, pltpu.HBM)
        for x in (write_pos, query_states, key_states, value_states, queue_keys, teacher)
    ]
    results = pl.pallas_call(
        whole_kernel,
        name="whole",
        out_shape=(
            pltpu.VMEM((1, 128), jnp.float32),
            pltpu.VMEM((1, HEADS * HD), jnp.float32),
            pltpu.VMEM(query_states.shape, jnp.bfloat16),
            pltpu.VMEM(key_states.shape, jnp.bfloat16),
            pltpu.VMEM(value_states.shape, jnp.bfloat16),
        ),
        in_specs=[in_hbm, anywhere] + [in_hbm] * 5,
        out_specs=(vmem, vmem, anywhere, vmem, anywhere),
        scratch_shapes=[
            pltpu.SMEM((DOCS,), jnp.int32),
            pltpu.SMEM((1,), jnp.int32),
            b16(2, BLOCK, WIDE),
            b16(4, BLOCK, KV),
            b16(4, BLOCK, KV),
            f32(DOCS, ENTRIES),
            f32(2, HALF, BLOCK, 3 * BLOCK),
            f32(4, HALF, BLOCK),
            f32(2, HALF, BLOCK),
            b16(2, GROUPS, 4 * BLOCK, 3 * BLOCK),
            b16(2, GROUPS, BLOCK, HD),
            b16(2, GROUPS, BLOCK, HD),
            f32(2, BLOCK, KV),
            f32(2, BLOCK, KV),
            b16(2, BLOCK, KV),
            b16(2, BLOCK, WIDE),
            b16(ENTRIES, 2048),
            f32(16, 128),
            f32(NZ, HALF, 128),
            f32(PLANE, HALF, 128),
            f32(DOCS, 2, 16, 128),
            f32(PLANE, 16, 128),
            f32(NZ, 16, 128),
            f32(16, 128),
            f32(HALF, 128),
            f32(DOCS, 2, 16, 128),
            f32(PLANE, 16, 128),
            f32(NZ, 16, 128),
            f32(HALF, 128),
            f32(HALF, 128),
            f32(16, 128),
            f32(HEADS, 128),
            f32(DOCS, HEADS, 128),
            f32(16, 128),
            pltpu.SemaphoreType.REGULAR((3,)),
            pltpu.SemaphoreType.DMA((7,)),
            pltpu.SemaphoreType.DMA((8,)),
            pltpu.SemaphoreType.DMA((8,)),
            pltpu.SemaphoreType.DMA((13,)),
            pltpu.SemaphoreType.DMA((13,)),
        ],
        compiler_params=pltpu.CompilerParams(
            collective_id=0, has_side_effects=True, vmem_limit_bytes=40 * 1024 * 1024
        ),
    )(held[0], lengths, *held[1:])
    loss, unit_vec, grad_query, grad_key, grad_value = finish(*results)
    return loss[0, 0], unit_vec, grad_query, grad_key, grad_value


def solution(mesh):
    placed = (
        P("grp", "ctx", None),
        P("grp", "ctx", None),
        P("grp", "ctx", None),
        P("grp"),
        P(("ctx", "grp"), None),
        P(),
        P(None, ("ctx", "grp")),
    )
    return jax.shard_map(
        shards,
        mesh=mesh,
        in_specs=placed,
        out_specs=(
            P(),
            P("grp", None),
            P("grp", "ctx", None),
            P("grp", "ctx", None),
            P("grp", "ctx", None),
        ),
        check_vma=False,
    )
```

```python
import functools

import jax
import jax.numpy as jnp
from jax import lax
from jax.experimental import pallas as pl
from jax.experimental.pallas import tpu as pltpu
from jax.sharding import PartitionSpec as P

HD = 128
HEADS = 16
GROUPS = 2
BLOCK = 128
KV = GROUPS * HD
CHIPS = 32
HALF = 8
WIDE = HALF * HD
DOCS = 8
ENTRIES = 256
NZ = 16
PLANE = 32
ROWS = 9

inverse_temp = 10.0
loss_scale = 2.0**24
norm_eps = 1e-06

MESH = pl.DeviceIdType.MESH


def position():
    ctx = lax.axis_index("ctx")
    grp = lax.axis_index("grp")
    return ctx // 32, (ctx // 2) % NZ, ctx % 2, grp


def device(x_hi, z, core, grp):
    return ((x_hi * NZ + z) * 2 + core, grp)


def shifted(dx=0, dy=0, dz=0, dc=0):
    x_hi, z, core, grp = position()
    x = (2 * x_hi + grp // 4 + dx) % 4
    return device(x // 2, (z + dz) % NZ, (core + dc) % 2, (x % 2) * 4 + (grp + dy) % 4)


def plane_peer(step):
    x_hi, z, core, grp = position()
    turn = (step // 4) % 4
    turn = turn + turn // 2 - 2 * (turn // 3)
    px = (x_hi + step // 16) % 2
    pc = (core + step % 2) % 2
    pl_x = (grp // 4 + (step // 2) % 2) % 2
    py = (grp + turn) % 4
    return px, pc, pl_x * 4 + py


def z_offset(step):
    return 8 + ((step + 1) // 2) * (2 * (step % 2) - 1)


def send_plane(src_of, dst, send_sem, recv_sem):
    x_hi, z, core, grp = position()
    mine = x_hi * 16 + core * 8 + grp

    def one(k):
        px, pc, pg = plane_peer(31 - k)
        pltpu.make_async_remote_copy(
            src_ref=src_of(pc, pg),
            dst_ref=dst(mine),
            send_sem=send_sem,
            recv_sem=recv_sem,
            device_id=device(px, z, pc, pg),
            device_id_type=MESH,
        ).start()

    for k in range(PLANE - 1):
        one(k)


def send_ring(src, dst, send_sem, recv_sem):
    x_hi, z, core, grp = position()

    def one(k):
        pltpu.make_async_remote_copy(
            src_ref=src,
            dst_ref=dst(z),
            send_sem=send_sem,
            recv_sem=recv_sem,
            device_id=device(x_hi, (z + z_offset(k)) % NZ, core, grp),
            device_id_type=MESH,
        ).start()

    for k in range(NZ - 1):
        one(k)


def wait_bytes(ref, sem):
    pltpu.make_async_copy(ref, ref, sem).wait()


def sum_slots(ref, count):
    total = ref[0]
    for i in range(1, count):
        total = total + ref[i]
    return total


def two_halves(x):
    high = x.astype(jnp.bfloat16).astype(jnp.float32)
    return jnp.concatenate([high, x - high], 0).astype(jnp.bfloat16)


def whole_kernel(
    pos_hbm, len_hbm, query_hbm, key_hbm, value_hbm, queue_ref, teacher_hbm,
    loss_ref, emb_ref, dq_ref, dk_ref, dv_ref,
    pos_ref, len_ref, query, keys, values, teacher_ref, prob, sums, sums_in, score,
    dk_out, dk_in, dk_chip, dk_part, dv_chip, dq_chip,
    eff, mix, zb, pb, t_out, tp, tz, t_own, t_half, s_out, ep, ez, half_sum, ring_out,
    t_ring_out, t_full, unit_rows, e_ring_out,
    ready, load_sem, send, recv, near_send, near_recv,
):
    x_hi, z, core, grp = position()
    mine = x_hi * 16 + core * 8 + grp
    ctx = (x_hi * NZ + z) * 2 + core
    chip = x_hi * NZ + z
    twin = (chip * 2 + 1 - core, grp)

    def beside(by, which):
        return ((chip + CHIPS + by) % CHIPS * 2 + which, grp)

    barrier = pltpu.get_barrier_semaphore()
    first = [shifted(dx=dx, dy=dy) for dx in (1, 3) for dy in (1, 3)]
    first += [shifted(dz=2), shifted(dz=NZ - 2), shifted(dx=2), shifted(dy=2)]
    first += [beside(by, which) for by in (1, -1) for which in (0, 1)]
    first += [shifted(dz=1), shifted(dz=NZ - 1), shifted(dx=1), shifted(dx=3), shifted(dy=1), shifted(dy=3), twin]
    for to in first:
        pl.semaphore_signal(barrier, inc=1, device_id=to, device_id_type=MESH)

    loads = []
    for i, (source, goal) in enumerate((
        (teacher_hbm, teacher_ref),
        (queue_ref, eff),
        (key_hbm.at[0, :, pl.ds(pl.multiple_of(core * KV, KV), KV)], keys.at[2 + core]),
        (query_hbm.at[0, :, pl.ds(pl.multiple_of(core * WIDE, WIDE), WIDE)], query.at[core]),
        (value_hbm.at[0, :, pl.ds(pl.multiple_of(core * KV, KV), KV)], values.at[2 + core]),
        (pos_hbm, pos_ref),
        (len_hbm, len_ref),
    )):
        loads.append(pltpu.make_async_copy(source, goal, load_sem.at[i]))
        loads[-1].start()

    pl.semaphore_wait(barrier, len(first))

    def start(source, goal, which, to):
        copy = pltpu.make_async_remote_copy(
            src_ref=source,
            dst_ref=goal,
            send_sem=near_send.at[which],
            recv_sem=near_recv.at[which],
            device_id=to,
            device_id_type=MESH,
        )
        copy.start()
        return copy

    def to_next(source, goal, which):
        for half in range(2):
            pltpu.make_async_remote_copy(
                src_ref=source.at[0, :, pl.ds(half * KV, KV)],
                dst_ref=goal.at[core],
                send_sem=near_send.at[which + half],
                recv_sem=near_recv.at[which + core],
                device_id=beside(1, half),
                device_id_type=MESH,
            ).start()

    other_kv = pl.ds(pl.multiple_of((1 - core) * KV, KV), KV)
    other_wide = pl.ds(pl.multiple_of((1 - core) * WIDE, WIDE), WIDE)
    to_next(key_hbm, keys, 0)
    start(key_hbm.at[0, :, other_kv], keys.at[2 + core], 2, twin)
    start(query_hbm.at[0, :, other_wide], query.at[core], 3, twin)
    start(value_hbm.at[0, :, other_kv], values.at[2 + core], 6, twin)
    to_next(value_hbm, values, 4)
    for to in (shifted(dz=2), shifted(dz=NZ - 2), shifted(dx=2), shifted(dy=2), twin):
        pl.semaphore_signal(ready.at[0], inc=1, device_id=to, device_id_type=MESH)

    base = (ctx * 8 + grp) * ENTRIES
    entry = lax.broadcasted_iota(jnp.int32, (DOCS, ENTRIES), 1) + base
    lane = lax.broadcasted_iota(jnp.int32, (DOCS, 128), 1)
    row = lax.broadcasted_iota(jnp.int32, (DOCS, 128), 0)
    loads[0].wait()
    loads[5].wait()
    loads[6].wait()
    teacher = teacher_ref[...]
    kept = jnp.ones((DOCS, ENTRIES), jnp.float32)
    there = jnp.zeros((DOCS, 128), jnp.float32)
    teacher_at = jnp.zeros((DOCS, 128), jnp.float32)
    for d in range(DOCS):
        hit = (entry == pos_ref[d]).astype(jnp.float32)
        kept = kept - hit
        at = (lane == d).astype(jnp.float32)
        there = there + at * jnp.sum(hit, 1, keepdims=True)
        teacher_at = teacher_at + at * jnp.sum(teacher * hit, 1, keepdims=True)
    target = jnp.where(kept > 0, jnp.exp(teacher), 0.0)
    target_at = jnp.where(there > 0, jnp.exp(teacher_at), 0.0)
    target_sum = jnp.sum(target, 1, keepdims=True) + jnp.sum(target_at, 1, keepdims=True)
    target_row = jnp.sum(jnp.where(lane == row, target_sum, 0.0), 0, keepdims=True) + pltpu.roll(target_at, DOCS, 1)

    def spread(out, part):
        for h in range(HEADS):
            out[:, h // HALF, h % HALF] = part[:, h * HD : (h + 1) * HD]

    loads[1].wait()
    mixed = jnp.dot(two_halves(target), eff[...], preferred_element_type=jnp.float32)
    spread(t_out, mixed[:DOCS] + mixed[DOCS:])
    for c in range(2):
        t_out[:, c, HALF] = target_row

    pl.semaphore_wait(ready.at[0], 5)
    pl.semaphore_signal(ready.at[1], inc=1, device_id=twin, device_id_type=MESH)
    for to in (4, NZ - 4):
        pl.semaphore_signal(ready.at[2], inc=1, device_id=shifted(dz=to), device_id_type=MESH)

    later = lax.broadcasted_iota(jnp.int32, (BLOCK, BLOCK), 1)
    rows = lax.broadcasted_iota(jnp.int32, (BLOCK, BLOCK), 0)
    inside = (later > rows, None, later <= rows)

    def stacked(r, g):
        return jnp.concatenate([query[r, :, (4 * g + j) * HD : (4 * g + j + 1) * HD] for j in range(4)], 0)

    def weigh(r, s):
        for g in range(GROUPS):
            tile = keys[r + s, :, g * HD : (g + 1) * HD]
            scores = lax.dot_general(
                stacked(r, g), tile, (((1,), (1,)), ((), ())), preferred_element_type=jnp.float32
            )
            weight = jnp.exp(scores * HD ** (-0.5)).reshape(4, BLOCK, BLOCK)
            seen = inside[s]
            if r + s < 2:
                before = jnp.broadcast_to(chip >= 1, (BLOCK, BLOCK))
                seen = before if seen is None else seen & before
            if seen is not None:
                weight = jnp.where(seen[None], weight, 0.0)
            prob[r, 4 * g : 4 * g + 4, :, s * BLOCK : (s + 1) * BLOCK] = weight

    def arrived(ref, which):
        wait_bytes(ref, near_recv.at[which])

    for i in (2, 3, 4):
        loads[i].wait()
    arrived(keys.at[0], 2)
    arrived(query.at[0], 3)
    weigh(0, 2)
    weigh(1, 1)
    weigh(1, 2)
    arrived(keys.at[0], 0)
    arrived(keys.at[0], 1)
    weigh(0, 0)
    weigh(0, 1)
    weigh(1, 0)

    length = len_ref[0]
    column = []
    for r in range(2):
        place = lax.broadcasted_iota(jnp.int32, (BLOCK, 1), 0) + (chip * 2 + r) * BLOCK
        live = (place < length).astype(jnp.float32)
        for h in range(HALF):
            weight = prob[r, h]
            total = weight[:, :BLOCK] + weight[:, BLOCK : 2 * BLOCK] + weight[:, 2 * BLOCK :]
            part = weight * (live / jnp.sum(total, 1, keepdims=True))
            prob[r, h] = part
            column.append(jnp.sum(part, 0, keepdims=True))
    for block in range(4):
        parts = []
        for r in range(2):
            s = block - r
            if 0 <= s < 3:
                parts.append(
                    jnp.concatenate([column[r * HALF + h][:, s * BLOCK : (s + 1) * BLOCK] for h in range(HALF)], 0)
                )
        sums[block] = parts[0] if len(parts) == 1 else parts[0] + parts[1]
    start(sums.at[pl.ds(0, 2)], sums_in, 7, beside(-1, core))

    pl.semaphore_wait(ready.at[1], 1)
    send_plane(
        lambda pc, pg: t_out.at[pg, pc, pl.ds(0, ROWS)],
        lambda me: tp.at[me, pl.ds(0, ROWS)],
        send.at[0],
        recv.at[0],
    )
    tp[mine] = t_out[grp, core]

    length_float = length.astype(jnp.float32)
    for which in (6, 4, 5):
        arrived(values.at[0], which)
    for g in range(GROUPS):
        both = jnp.concatenate([sums[b, 4 * g : 4 * g + 4] for b in range(4)], 1)
        split = jnp.concatenate([both, jnp.zeros_like(both)], 0)
        tile = values[:, :, g * HD : (g + 1) * HD].reshape(4 * BLOCK, HD)
        out = jnp.dot(two_halves(split), tile, preferred_element_type=jnp.float32)
        half_sum[4 * g : 4 * g + 4] = (out[:4] + out[8:12]) / length_float

    pl.semaphore_wait(ready.at[2], 2)
    send_ring(half_sum, lambda me: zb.at[me], send.at[2], recv.at[2])
    zb[z] = half_sum[...]

    wait_bytes(tp.at[pl.ds(0, PLANE - 1), pl.ds(0, ROWS)], recv.at[0])
    t_ring_out[...] = sum_slots(tp, PLANE)

    wait_bytes(zb.at[pl.ds(0, NZ - 1)], recv.at[2])
    ring_out[...] = sum_slots(zb, NZ)
    send_plane(lambda pc, pg: ring_out, lambda me: pb.at[me], send.at[4], recv.at[4])
    pb[mine] = ring_out[...]
    send_ring(t_ring_out.at[pl.ds(0, ROWS)], lambda me: tz.at[me, pl.ds(0, ROWS)], send.at[3], recv.at[3])
    tz[z] = t_ring_out[...]

    wait_bytes(pb.at[pl.ds(0, PLANE - 1)], recv.at[4])
    heads = []
    for c in range(2):
        both = pb[pl.ds(c * 8, 8)] + pb[pl.ds(16 + c * 8, 8)]
        unit_rows[:, pl.ds(c * HALF, HALF)] = both
    square = jnp.zeros((DOCS, HD), jnp.float32)
    for h in range(HEADS):
        tile = unit_rows[:, h]
        heads.append(tile)
        square = square + tile * tile
    root_mean = jnp.sqrt(jnp.sum(square, 1, keepdims=True) / 2048.0 + norm_eps)
    norm_scale = root_mean * 2048.0**0.5
    unit = [(heads[h] / norm_scale).astype(jnp.bfloat16) for h in range(HEADS)]
    unit16 = jnp.concatenate(unit, 1)
    unit16 = jnp.concatenate([unit16, jnp.zeros_like(unit16)], 0)
    near = (
        lax.dot_general(unit16, eff[...], (((1,), (1,)), ((), ())), preferred_element_type=jnp.float32)[:DOCS]
        * inverse_temp
    )
    unit = [x.astype(jnp.float32) for x in unit]
    far = jnp.zeros((DOCS, 128), jnp.float32)
    for d in range(DOCS):
        product = unit[0] * unit[0][d : d + 1]
        for h in range(1, HEADS):
            product = product + unit[h] * unit[h][d : d + 1]
        far = far + jnp.where(lane == d, inverse_temp * jnp.sum(product, 1, keepdims=True), 0.0)
    student = jnp.where(kept > 0, jnp.exp(near), 0.0)
    student_at = jnp.where(there > 0, jnp.exp(far), 0.0)
    student_sum = jnp.sum(student, 1, keepdims=True) + jnp.sum(student_at, 1, keepdims=True)
    cross = jnp.sum(target * (teacher - near), 1, keepdims=True) + jnp.sum(
        target_at * (teacher_at - far), 1, keepdims=True
    )
    inner = jnp.sum(student * near, 1, keepdims=True) + jnp.sum(student_at * far, 1, keepdims=True)
    extra = jnp.zeros((DOCS, 128), jnp.float32)
    for i, value in enumerate((student_sum, cross, inner)):
        extra = extra + jnp.where(lane == row + DOCS * i, value, 0.0)
    extra = jnp.broadcast_to(jnp.sum(extra, 0, keepdims=True), (DOCS, 128))
    mixed = jnp.dot(two_halves(student), eff[...], preferred_element_type=jnp.float32)
    weights = [jnp.sum(jnp.where(lane == d, student_at, 0.0), 1, keepdims=True) for d in range(DOCS)]
    for h in range(HEADS):
        tile = mixed[:DOCS, h * HD : (h + 1) * HD] + mixed[DOCS:, h * HD : (h + 1) * HD]
        for d in range(DOCS):
            tile = tile + weights[d] * unit[h][d : d + 1]
        s_out[:, h // HALF, h % HALF] = tile
    for c in range(2):
        s_out[:, c, HALF] = extra
    send_plane(
        lambda pc, pg: s_out.at[pg, pc, pl.ds(0, ROWS)], lambda me: ep.at[me, pl.ds(0, ROWS)], send.at[6], recv.at[6]
    )
    ep[mine] = s_out[grp, core]

    wait_bytes(tz.at[pl.ds(0, NZ - 1), pl.ds(0, ROWS)], recv.at[3])
    t_own[...] = sum_slots(tz, NZ)
    t_pair = pltpu.make_async_remote_copy(
        src_ref=t_own.at[pl.ds(0, HALF)],
        dst_ref=t_half,
        send_sem=send.at[5],
        recv_sem=recv.at[5],
        device_id=twin,
        device_id_type=MESH,
    )
    t_pair.start()

    own = unit_rows[grp]
    own_mean = jnp.sqrt(jnp.sum(jnp.sum(own * own, 1, keepdims=True), 0, keepdims=True) / 2048.0 + norm_eps)
    own_scale = own_mean * 2048.0**0.5
    emb = own / own_scale
    for h in range(HEADS):
        emb_ref[:, h * HD : (h + 1) * HD] = emb[h : h + 1]
    emb_half = unit_rows[grp, pl.ds(pl.multiple_of(core * HALF, HALF), HALF)] / own_scale
    t_pair.wait_recv()
    t_full[pl.ds(pl.multiple_of(core * HALF, HALF), HALF)] = t_own[pl.ds(0, HALF)]
    t_full[pl.ds(pl.multiple_of((1 - core) * HALF, HALF), HALF)] = t_half[...]
    t_sum = t_full[...]
    lane1 = lax.broadcasted_iota(jnp.int32, (1, 128), 1)
    target_row = t_own[pl.ds(HALF, 1)]
    for d in range(DOCS):
        weight = jnp.sum(jnp.where(lane1 == DOCS + d, target_row, 0.0), 1, keepdims=True)
        other = unit_rows[d]
        other_mean = jnp.sqrt(jnp.sum(jnp.sum(other * other, 1, keepdims=True), 0, keepdims=True) / 2048.0 + norm_eps)
        other_unit = (other / (other_mean * 2048.0**0.5)).astype(jnp.bfloat16).astype(jnp.float32)
        t_sum = t_sum + weight * other_unit
    target_total = jnp.sum(jnp.where(lane1 == grp, target_row, 0.0), 1, keepdims=True)
    unit_own = emb.astype(jnp.bfloat16).astype(jnp.float32)
    t_inner = jnp.sum(jnp.sum(unit_own * t_sum, 1, keepdims=True), 0, keepdims=True) / target_total
    t_full[...] = t_sum
    t_mean = t_full[pl.ds(pl.multiple_of(core * HALF, HALF), HALF)] / target_total
    mine_only = lax.broadcasted_iota(jnp.int32, (HALF, KV), 1) // HD == (
        lax.broadcasted_iota(jnp.int32, (HALF, KV), 0) // 4
    )
    arrived(sums_in, 7)
    sums_all = sums[pl.ds(2, 2)] + sums_in[...]

    wait_bytes(ep.at[pl.ds(0, PLANE - 1), pl.ds(0, ROWS)], recv.at[6])
    e_ring_out[...] = sum_slots(ep, PLANE)
    send_ring(e_ring_out.at[pl.ds(0, ROWS)], lambda me: ez.at[me, pl.ds(0, ROWS)], send.at[7], recv.at[7])
    ez[z] = e_ring_out[...]
    wait_bytes(ez.at[pl.ds(0, NZ - 1), pl.ds(0, ROWS)], recv.at[7])
    mix[...] = sum_slots(ez, NZ)
    student_all = mix[pl.ds(HALF, 1)]
    cross_all = pltpu.roll(student_all, 128 - DOCS, 1)
    student_total = jnp.sum(jnp.where(lane1 == grp, student_all, 0.0), 1, keepdims=True)
    s_inner = jnp.sum(jnp.where(lane1 == grp + 2 * DOCS, student_all, 0.0), 1, keepdims=True) / (
        inverse_temp * student_total
    )
    factor = inverse_temp * loss_scale / DOCS
    unit_grad = factor * (mix[pl.ds(0, HALF)] / student_total - t_mean)
    cot = (unit_grad - emb_half * (factor * (s_inner - t_inner))) / own_scale / length_float
    cot_diag = jnp.where(mine_only, jnp.concatenate([cot] * GROUPS, 1), 0.0)
    cot_diag = jnp.concatenate([cot_diag, jnp.zeros_like(cot_diag)], 0).astype(jnp.bfloat16)
    prob_grad = lax.dot_general(
        cot_diag, values[...].reshape(4 * BLOCK, KV), (((1,), (1,)), ((), ())), preferred_element_type=jnp.float32
    )

    def scored(r, g):
        for h in range(4 * g, 4 * g + 4):
            part = prob[r, h]
            push = part * prob_grad[h : h + 1, r * BLOCK : (r + 3) * BLOCK]
            total = push[:, :BLOCK] + push[:, BLOCK : 2 * BLOCK] + push[:, 2 * BLOCK :]
            score[r, g, (h % 4) * BLOCK : (h % 4 + 1) * BLOCK] = (
                push - part * jnp.sum(total, 1, keepdims=True)
            ).astype(jnp.bfloat16)

    def key_grad(block, g):
        total = None
        for r in range(2):
            s = block - r
            if 0 <= s < 3:
                one = lax.dot_general(
                    score[r, g, :, s * BLOCK : (s + 1) * BLOCK],
                    stacked(r, g),
                    (((0,), (0,)), ((), ())),
                    preferred_element_type=jnp.float32,
                )
                total = one if total is None else total + one
        return total * HD ** (-0.5)

    def send_back(block, g):
        dk_out[block, g] = key_grad(block, g).astype(jnp.bfloat16)
        pltpu.make_async_remote_copy(
            src_ref=dk_out.at[block, g],
            dst_ref=dk_in.at[core, g],
            send_sem=near_send.at[8 + block],
            recv_sem=near_recv.at[8 + core],
            device_id=beside(-1, block),
            device_id_type=MESH,
        ).start()

    def query_grad(r):
        for g in range(GROUPS):
            tile = keys[pl.ds(r, 3), :, g * HD : (g + 1) * HD].reshape(3 * BLOCK, HD)
            dq = jnp.dot(score[r, g], tile, preferred_element_type=jnp.float32) * HD ** (-0.5)
            for j in range(4):
                h = 4 * g + j
                dq_chip[r, :, h * HD : (h + 1) * HD] = dq[j * BLOCK : (j + 1) * BLOCK].astype(jnp.bfloat16)

    for r in range(2):
        for g in range(GROUPS):
            scored(r, g)
            send_back(r, g)
    own_wide = pl.ds(pl.multiple_of(core * WIDE, WIDE), WIDE)
    own_kv = pl.ds(pl.multiple_of(core * KV, KV), KV)
    query_grad(1 - core)
    start(dq_chip.at[1 - core], dq_ref.at[0, :, own_wide], 10, twin)
    for block in range(2):
        for g in range(GROUPS):
            dk_chip[block, :, g * HD : (g + 1) * HD] = key_grad(2 + block, g)
    start(dk_chip.at[1 - core], dk_part.at[core], 11, twin)
    for block in range(2):
        high = sums_all[block].astype(jnp.bfloat16).astype(jnp.float32)
        dv_chip[block] = lax.dot_general(
            jnp.concatenate([high, sums_all[block] - high], 0).astype(jnp.bfloat16),
            jnp.concatenate([cot_diag[:HALF], cot_diag[:HALF]], 0),
            (((0,), (0,)), ((), ())),
            preferred_element_type=jnp.float32,
        ).astype(jnp.bfloat16)
    start(dv_chip.at[1 - core], dv_ref.at[0, :, own_kv], 12, twin)
    query_grad(core)
    stays = [
        pltpu.make_async_copy(dq_chip.at[core], dq_ref.at[0, :, own_wide], load_sem.at[0]),
        pltpu.make_async_copy(dv_chip.at[core], dv_ref.at[0, :, own_kv], load_sem.at[1]),
    ]
    for copy in stays:
        copy.start()
    dk_part[core] = dk_chip[core]
    terms = jnp.where(
        lane1 < DOCS,
        cross_all / jnp.where(lane1 < DOCS, target_row, 1.0)
        - jnp.log(jnp.where(lane1 < DOCS, target_row, 1.0))
        + jnp.log(jnp.where(lane1 < DOCS, student_all, 1.0)),
        0.0,
    )
    loss_ref[...] = jnp.broadcast_to(jnp.sum(terms, 1, keepdims=True) / DOCS, (1, 128))
    arrived(dk_chip.at[0], 11)
    for half in range(2):
        arrived(dk_out.at[0], 8 + half)
        arrived_part = jnp.concatenate([dk_in[half, g] for g in range(GROUPS)], 1).astype(jnp.float32)
        dk_ref[0, :, half * KV : (half + 1) * KV] = (dk_part[half] + arrived_part).astype(jnp.bfloat16)

    arrived(dq_chip.at[0], 10)
    arrived(dv_chip.at[0], 12)
    for copy in stays:
        copy.wait()
    for ref, which in (
        (keys.at[0], 0), (keys.at[0], 1), (keys.at[0], 2), (query.at[0], 3), (values.at[0], 4),
        (values.at[0], 5), (values.at[0], 6), (sums_in, 7), (dk_out.at[0], 8), (dk_out.at[0], 9),
        (dq_chip.at[0], 10), (dk_chip.at[0], 11), (dv_chip.at[0], 12),
    ):
        wait_bytes(ref, near_send.at[which])
    wait_bytes(tp.at[pl.ds(0, PLANE - 1), pl.ds(0, ROWS)], send.at[0])
    wait_bytes(zb.at[pl.ds(0, NZ - 1)], send.at[2])
    wait_bytes(tz.at[pl.ds(0, NZ - 1), pl.ds(0, ROWS)], send.at[3])
    wait_bytes(pb.at[pl.ds(0, PLANE - 1)], send.at[4])
    t_pair.wait_send()
    wait_bytes(ep.at[pl.ds(0, PLANE - 1), pl.ds(0, ROWS)], send.at[6])
    wait_bytes(ez.at[pl.ds(0, NZ - 1), pl.ds(0, ROWS)], send.at[7])


def finish_kernel(loss_in, emb_in, dq_in, dk_in, dv_in, loss_out, emb_out, dq_out, dk_out, dv_out, loss_here, sem):
    pairs = ((dq_in, dq_out), (dk_in, dk_out), (dv_in, dv_out), (emb_in, emb_out), (loss_here, loss_out))
    loss_here[...] = loss_in[:, :1]
    copies = [pltpu.make_async_copy(source, goal, sem.at[i]) for i, (source, goal) in enumerate(pairs)]
    for copy in copies:
        copy.start()
    for copy in copies:
        copy.wait()


def finish(loss, *arrays):
    vmem = pl.BlockSpec(memory_space=pltpu.VMEM)
    shapes = [jax.ShapeDtypeStruct((1, 1), jnp.float32)] + [jax.ShapeDtypeStruct(x.shape, x.dtype) for x in arrays]
    return pl.pallas_call(
        finish_kernel,
        name="finish",
        out_shape=tuple(shapes),
        in_specs=[vmem] * 5,
        out_specs=(pl.BlockSpec(memory_space=pl.ANY),) * 5,
        scratch_shapes=[pltpu.VMEM((1, 1), jnp.float32), pltpu.SemaphoreType.DMA((5,))],
        compiler_params=pltpu.CompilerParams(vmem_limit_bytes=4 * 1024 * 1024),
    )(loss, *arrays)


def shards(query_states, key_states, value_states, lengths, queue_keys, write_pos, teacher):
    vmem = pl.BlockSpec(memory_space=pltpu.VMEM)
    in_hbm = pl.BlockSpec(memory_space=pltpu.HBM)
    anywhere = pl.BlockSpec(memory_space=pl.ANY)

    def f32(*shape):
        return pltpu.VMEM(shape, jnp.float32)

    def b16(*shape):
        return pltpu.VMEM(shape, jnp.bfloat16)

    held = [
        pltpu.with_memory_space_constraint(x, pltpu.HBM)
        for x in (write_pos, query_states, key_states, value_states, queue_keys, teacher)
    ]
    results = pl.pallas_call(
        whole_kernel,
        name="whole",
        out_shape=(
            pltpu.VMEM((1, 128), jnp.float32),
            pltpu.VMEM((1, HEADS * HD), jnp.float32),
            pltpu.VMEM(query_states.shape, jnp.bfloat16),
            pltpu.VMEM(key_states.shape, jnp.bfloat16),
            pltpu.VMEM(value_states.shape, jnp.bfloat16),
        ),
        in_specs=[in_hbm, anywhere] + [in_hbm] * 5,
        out_specs=(vmem, vmem, anywhere, vmem, anywhere),
        scratch_shapes=[
            pltpu.SMEM((DOCS,), jnp.int32),
            pltpu.SMEM((1,), jnp.int32),
            b16(2, BLOCK, WIDE),
            b16(4, BLOCK, KV),
            b16(4, BLOCK, KV),
            f32(DOCS, ENTRIES),
            f32(2, HALF, BLOCK, 3 * BLOCK),
            f32(4, HALF, BLOCK),
            f32(2, HALF, BLOCK),
            b16(2, GROUPS, 4 * BLOCK, 3 * BLOCK),
            b16(2, GROUPS, BLOCK, HD),
            b16(2, GROUPS, BLOCK, HD),
            f32(2, BLOCK, KV),
            f32(2, BLOCK, KV),
            b16(2, BLOCK, KV),
            b16(2, BLOCK, WIDE),
            b16(ENTRIES, 2048),
            f32(16, 128),
            f32(NZ, HALF, 128),
            f32(PLANE, HALF, 128),
            f32(DOCS, 2, 16, 128),
            f32(PLANE, 16, 128),
            f32(NZ, 16, 128),
            f32(16, 128),
            f32(HALF, 128),
            f32(DOCS, 2, 16, 128),
            f32(PLANE, 16, 128),
            f32(NZ, 16, 128),
            f32(HALF, 128),
            f32(HALF, 128),
            f32(16, 128),
            f32(HEADS, 128),
            f32(DOCS, HEADS, 128),
            f32(16, 128),
            pltpu.SemaphoreType.REGULAR((3,)),
            pltpu.SemaphoreType.DMA((7,)),
            pltpu.SemaphoreType.DMA((8,)),
            pltpu.SemaphoreType.DMA((8,)),
            pltpu.SemaphoreType.DMA((13,)),
            pltpu.SemaphoreType.DMA((13,)),
        ],
        compiler_params=pltpu.CompilerParams(
            collective_id=0, has_side_effects=True, vmem_limit_bytes=40 * 1024 * 1024
        ),
    )(held[0], lengths, *held[1:])
    loss, unit_vec, grad_query, grad_key, grad_value = finish(*results)
    return loss[0, 0], unit_vec, grad_query, grad_key, grad_value


def solution(mesh):
    placed = (
        P("grp", "ctx", None),
        P("grp", "ctx", None),
        P("grp", "ctx", None),
        P("grp"),
        P(("ctx", "grp"), None),
        P(),
        P(None, ("ctx", "grp")),
    )
    return jax.shard_map(
        shards,
        mesh=mesh,
        in_specs=placed,
        out_specs=(
            P(),
            P("grp", None),
            P("grp", "ctx", None),
            P("grp", "ctx", None),
            P("grp", "ctx", None),
        ),
        check_vma=False,
    )
```
